512 devices in a mesh: dp: 4 (over y), ctx: 32 (over x, z_lo), tp: 4 (over z_hi, core).
Axes of the slice: x: 4, y: 4, z: 16 (z_hi: 2, z_lo: 8; z = z_hi * 8 + z_lo), core: 2. Of those that a mesh axis runs over, the one named last changes fastest.
Arguments:
- queries: bfloat16 [4, 4096, 4096], P('dp', 'ctx', 'tp'), may hold values from -6 to 6
- keys: bfloat16 [4, 4096, 512], P('dp', 'ctx', 'tp'), may hold values from -6 to 6
- values: bfloat16 [4, 4096, 512], P('dp', 'ctx', 'tp'), may hold values from -6 to 6
- out_grad: bfloat16 [4, 4096, 4096], P('dp', 'ctx', 'tp'), may hold values from -6 to 6
- mixed_grad: bfloat16 [16384, 2048], P(('dp', 'ctx'), 'tp'), may hold values from -6 to 6
- expert_ids: int32 [16384, 8], P(('dp', 'ctx')), may hold values from 0 to 127, all different within a row; in each aligned block of 128 rows (0 to 127, 128 to 255, ...) at most 10 rows name the same one
- combine: bfloat16 [16384, 8], P(('dp', 'ctx')), may hold values from 0.049804688 to 1
- w_down: bfloat16 [128, 1536, 2048], P(('dp', 'ctx'), 'tp'), may hold values from -0.125 to 0.125
Outputs:
- query_grad: bfloat16 [4, 4096, 4096], P('dp', 'ctx', 'tp')
- key_grad: bfloat16 [4, 4096, 512], P('dp', 'ctx', 'tp')
- value_grad: bfloat16 [4, 4096, 512], P('dp', 'ctx', 'tp')
- hidden_grad: bfloat16 [128, 128, 10, 1536], P(('dp', 'ctx'), None, None, 'tp')
The draws below stay inside these ranges and needn't reach their ends.
Inputs may be any that keep to these rules, and one draw needn't show every extreme that they name: `expert_ids`: each row names 8 distinct experts. Within each aligned block of 128 rows no expert is named more than 10 times, a bound that some block reaches.
All inputs are finite; a program needn't handle non-finite values.
Results may differ from the reference program's by a relative error of at most 0.0071.
Values may be sent and summed in bfloat16 or wider, within the bound.
A program may use at most 128 MiB of HBM per device.

```python
import math
import jax
import jax.numpy as jnp
import numpy as np
from jax import lax

TOK_DEV = 128
HEADS = 32
KV_HEADS = 4
HEAD_DIM = 128
FEAT = 2048
HID = 1536
TOPK = 8
EXPERTS = 128
MOST = 10
SEQS = 4
LEN = 4096
TOKENS = 16384


def draw_queries(key, part):
    key = jax.random.fold_in(key, 11)
    group = HEADS // KV_HEADS
    shape = (SEQS, LEN, KV_HEADS, group, HEAD_DIM)
    drawn = jax.random.truncated_normal(key, -6.0, 6.0, shape, jnp.float32)
    return drawn.reshape(SEQS, LEN, HEADS * HEAD_DIM).astype(jnp.bfloat16)


def draw_keys(key, part):
    key = jax.random.fold_in(key, 23)
    shape = (SEQS, LEN, KV_HEADS, HEAD_DIM)
    drawn = jax.random.truncated_normal(key, -6.0, 6.0, shape, jnp.float32)
    return drawn.reshape(SEQS, LEN, KV_HEADS * HEAD_DIM).astype(jnp.bfloat16)


def block_levels(stream_key, dims, shards, smallest, largest):
    gain, own = 1.0, jax.random.fold_in(stream_key, 6)
    for dim, parts in shards:
        heights = jnp.exp(jax.random.uniform(jax.random.fold_in(own, dim), (parts,), jnp.float32, smallest / len(shards), largest / len(shards)))
        gain = gain * jnp.repeat(heights, dims[dim] // parts).reshape([-1 if axis == dim else 1 for axis in range(len(dims))])
    return gain


def assign_block(key, own, number, rows, count, top, bound, lean):
    ranking = jax.random.permutation(key, count)
    crowded, usual = portions_of(count, rows * top, bound, lean, True), portions_of(count, rows * top, bound, lean, False)
    places = jnp.arange(count)

    def named(tallies, offset_by):
        used = int((tallies > 0).sum())
        fixed = max(1, used // 4)
        passed = fixed + (places - fixed + offset_by * (used - fixed)) % max(1, count - fixed)
        return jnp.zeros((count,), jnp.int32).at[ranking[jnp.where(places < fixed, places, passed)]].set(jnp.asarray(tallies, jnp.int32))

    tallies = jnp.where(number % 4 == 0, named(crowded, number // 4), named(usual, number - number // 4 - 1))
    mixed = jax.random.permutation(jax.random.fold_in(own, 3), count)
    source_of, receiver = mixed[0:count // 2 * 2:2], mixed[1:count // 2 * 2:2]
    slack = jnp.minimum(tallies[source_of] - 1, bound - tallies[receiver]) // 2
    slack = jnp.where((source_of == ranking[0]) | (receiver == ranking[0]) | (tallies[receiver] == 0), 0, jnp.maximum(slack, 0))
    passed = jax.random.randint(jax.random.fold_in(own, 4), (count // 2,), 0, 1 << 20) % (slack + 1)
    tallies = tallies.at[source_of].add(-passed).at[receiver].add(passed)
    labels = jnp.searchsorted(jnp.cumsum(tallies), jnp.arange(rows * top), side="right").astype(jnp.int32)
    listing = labels.reshape(top, rows).T
    listing = listing[jax.random.permutation(jax.random.fold_in(own, 1), rows)]
    offset_by = jax.random.randint(jax.random.fold_in(own, 2), (rows, 1), 0, top)
    return jnp.take_along_axis(listing, (jnp.arange(top)[None, :] + offset_by) % top, axis=1)


def portions_of(number_of, total, reach, slope, full):
    portions = [(1 << 20) // math.isqrt(grade ** slope) + 1 for grade in range(1, number_of + 1)]
    largest = reach if full else min(reach, max(-(-total // number_of), total * portions[0] // sum(portions)))
    least = 1 if total - largest >= number_of - 1 else 0
    given, spare = [largest] + [least] * (number_of - 1), total - largest - least * (number_of - 1)
    while spare > 0:
        candidates = [i for i in range(1, number_of) if given[i] < largest] or [i for i in range(1, number_of) if given[i] < reach]
        pool, remaining = sum([portions[i] for i in candidates]), spare
        for i in candidates:
            addition = min(reach - given[i], max(1, remaining * portions[i] // pool), spare)
            given[i] = given[i] + addition
            spare = spare - addition
    return np.array(given)


def scatter_about(stream_key, shape, deviation, limit, shards=(), held_as=jnp.bfloat16):
    array = jax.random.normal(stream_key, shape, jnp.float32) * deviation
    if len(shards) > 0:
        array = block_levels(stream_key, shape, shards, -0.22, 0.18) * array
    return jnp.clip(array, min=-limit, max=limit).astype(held_as)


def setup_inputs(seed: int = 0) -> dict:
    key_of = jax.random.split(jax.random.key(seed), 9)
    queries = draw_queries(jax.random.fold_in(key_of[8], 71), 0)
    keys = draw_keys(jax.random.fold_in(key_of[8], 71), 0)
    values = scatter_about(key_of[2], (SEQS, LEN, KV_HEADS * HEAD_DIM), 1.0, 6.0, ((0, 4), (1, 32), (2, 4)))
    out_grad = scatter_about(key_of[3], (SEQS, LEN, HEADS * HEAD_DIM), 1.0, 6.0, ((0, 4), (1, 32), (2, 4)))
    mixed_grad = scatter_about(key_of[4], (TOKENS, FEAT), 1.0, 6.0, ((0, 128), (1, 4)))
    expert_ids_keys = jax.random.split(jax.random.fold_in(key_of[5], 1), TOKENS // TOK_DEV)
    expert_ids_turns = jax.random.permutation(jax.random.fold_in(key_of[5], 3), TOKENS // TOK_DEV)
    expert_ids = jax.vmap(lambda own, number: assign_block(jax.random.fold_in(key_of[5], 2), own, number, TOK_DEV, EXPERTS, TOPK, MOST, 2))(expert_ids_keys, expert_ids_turns).reshape((TOKENS, TOPK))
    combine = jnp.clip(jnp.exp(math.log(1.0) - 2.9996462 * jax.random.uniform(key_of[6], (TOKENS, TOPK), jnp.float32) ** block_levels(key_of[6], (TOKENS, TOPK), ((0, 128),), -0.2, 0.2)), 0.049804688, 1.0).astype(jnp.bfloat16)
    w_down = scatter_about(key_of[7], (EXPERTS, HID, FEAT), FEAT ** -0.5, 0.125, ((0, 128), (1, 4)))
    return dict(queries=queries, keys=keys, values=values, out_grad=out_grad, mixed_grad=mixed_grad, expert_ids=expert_ids, combine=combine, w_down=w_down)


def group_backward(operands):
    query_heads, grad_heads, key_rows, value_rows = operands
    score_scale = HEAD_DIM ** -0.5
    places = jnp.arange(LEN, dtype=jnp.int32)
    allowed = places[None, :] <= places[:, None]

    def one_head(carry, pair):
        key_total, value_total = carry
        query_rows, grad_rows = pair
        scores = jnp.dot(query_rows, key_rows.T, preferred_element_type=jnp.float32) * score_scale
        scores = jnp.where(allowed, scores, -jnp.inf)
        log_total = jax.nn.logsumexp(scores, axis=1, keepdims=True)
        probs = jnp.where(allowed, jnp.exp(scores - log_total), 0.0)
        grads = jnp.dot(grad_rows, value_rows.T, preferred_element_type=jnp.float32)
        delta = jnp.sum(probs * grads, axis=1, keepdims=True)
        dscore = probs * (grads - delta)
        probs_low = probs.astype(jnp.bfloat16)
        dscore_low = dscore.astype(jnp.bfloat16)
        query_part = (jnp.dot(dscore_low, key_rows, preferred_element_type=jnp.float32) * score_scale).astype(jnp.bfloat16)
        key_total = key_total + jnp.dot(dscore_low.T, query_rows, preferred_element_type=jnp.float32)
        value_total = value_total + jnp.dot(probs_low.T, grad_rows, preferred_element_type=jnp.float32)
        return (key_total, value_total), query_part

    start_totals = (jnp.zeros((LEN, HEAD_DIM), jnp.float32), jnp.zeros((LEN, HEAD_DIM), jnp.float32))
    (key_total, value_total), query_parts = lax.scan(one_head, start_totals, (query_heads, grad_heads))
    return query_parts, (key_total * score_scale).astype(jnp.bfloat16), value_total.astype(jnp.bfloat16)


def attention_backward(queries, keys, values, out_grad):
    group = HEADS // KV_HEADS
    query_groups = queries.reshape(SEQS, LEN, KV_HEADS, group, HEAD_DIM).transpose(0, 2, 3, 1, 4).reshape(SEQS * KV_HEADS, group, LEN, HEAD_DIM)
    grad_groups = out_grad.reshape(SEQS, LEN, KV_HEADS, group, HEAD_DIM).transpose(0, 2, 3, 1, 4).reshape(SEQS * KV_HEADS, group, LEN, HEAD_DIM)
    key_groups = keys.reshape(SEQS, LEN, KV_HEADS, HEAD_DIM).transpose(0, 2, 1, 3).reshape(SEQS * KV_HEADS, LEN, HEAD_DIM)
    value_groups = values.reshape(SEQS, LEN, KV_HEADS, HEAD_DIM).transpose(0, 2, 1, 3).reshape(SEQS * KV_HEADS, LEN, HEAD_DIM)
    query_parts, key_parts, value_parts = lax.map(group_backward, (query_groups, grad_groups, key_groups, value_groups))
    query_grad = query_parts.reshape(SEQS, KV_HEADS, group, LEN, HEAD_DIM).transpose(0, 3, 1, 2, 4).reshape(SEQS, LEN, HEADS * HEAD_DIM)
    key_grad = key_parts.reshape(SEQS, KV_HEADS, LEN, HEAD_DIM).transpose(0, 2, 1, 3).reshape(SEQS, LEN, KV_HEADS * HEAD_DIM)
    value_grad = value_parts.reshape(SEQS, KV_HEADS, LEN, HEAD_DIM).transpose(0, 2, 1, 3).reshape(SEQS, LEN, KV_HEADS * HEAD_DIM)
    return query_grad, key_grad, value_grad


def expert_backward(mixed_grad, expert_ids, combine, w_down):
    blocks = TOKENS // TOK_DEV
    entries = TOK_DEV * TOPK
    id_blocks = expert_ids.reshape(blocks, entries)
    weight_blocks = combine.reshape(blocks, entries).astype(jnp.float32)
    row_blocks = mixed_grad.reshape(blocks, TOK_DEV, FEAT).astype(jnp.float32)
    slot_places = jnp.arange(MOST, dtype=jnp.int32)

    def one_expert(pair):
        expert, weights = pair
        hits = (id_blocks == expert).astype(jnp.int32)
        ranks = jnp.cumsum(hits, axis=1) - 1
        chosen = ((hits[:, None, :] == 1) & (ranks[:, None, :] == slot_places[None, :, None])).astype(jnp.float32)
        token_pick = chosen.reshape(blocks, MOST, TOK_DEV, TOPK).sum(axis=3)
        rows = jnp.einsum("bct,btf->bcf", token_pick, row_blocks)
        slot_weights = jnp.einsum("bce,be->bc", chosen, weight_blocks)
        hidden = jnp.einsum("bcf,hf->bch", rows, weights.astype(jnp.float32))
        return (hidden * slot_weights[:, :, None]).astype(jnp.bfloat16)

    return lax.map(one_expert, (jnp.arange(EXPERTS, dtype=jnp.int32), w_down))


def reference(queries, keys, values, out_grad, mixed_grad, expert_ids, combine, w_down):
    query_grad, key_grad, value_grad = attention_backward(queries, keys, values, out_grad)
    hidden_grad = expert_backward(mixed_grad, expert_ids, combine, w_down)
    return (query_grad, key_grad, value_grad, hidden_grad)
```

```python
import functools
import math

import jax
import jax.numpy as jnp
from jax import lax
from jax.experimental import pallas as pl
from jax.experimental.pallas import tpu as pltpu
from jax.sharding import PartitionSpec as P

MESH = pl.DeviceIdType.MESH
HEAD_DIM = 128
GROUP = 8
TOK = 128
SLOTS = 10
EXPERTS = 128
NX, NY, NL, NZ = 4, 4, 8, 16
RUN = NL * TOK
WIDE = 2 * HEAD_DIM
CHUNK = 256
ROWS = GROUP * TOK
PACK = NL * SLOTS
SCALE = HEAD_DIM**-0.5
SCALE2 = SCALE / math.log(2.0)
MASKED = -1e30
F32, BF16 = jnp.float32, jnp.bfloat16


def dot_nt(a, b):
    return lax.dot_general(a, b, (((1,), (1,)), ((), ())), preferred_element_type=F32)


def dot_nn(a, b):
    return lax.dot_general(a, b, (((1,), (0,)), ((), ())), preferred_element_type=F32)


def dot_tn(a, b):
    return lax.dot_general(a, b, (((0,), (0,)), ((), ())), preferred_element_type=F32)


def remote(src, dst, sems, where):
    return pltpu.make_async_remote_copy(
        src_ref=src,
        dst_ref=dst,
        send_sem=sems[0],
        recv_sem=sems[1],
        device_id=where,
        device_id_type=MESH,
    )


def token_targets(ids_ref, comb_ref):
    expert = lax.broadcasted_iota(jnp.int32, (EXPERTS, TOK), 0)
    hits = jnp.zeros((EXPERTS, TOK), F32)
    for k in range(8):
        hits += jnp.where(ids_ref[k : k + 1, :] == expert, 1.0, 0.0)
    rows = lax.broadcasted_iota(jnp.int32, (TOK, TOK), 0)
    cols = lax.broadcasted_iota(jnp.int32, (TOK, TOK), 1)
    before = jnp.where(rows < cols, 1.0, 0.0).astype(BF16)
    ranks = dot_nn(hits.astype(BF16), before)
    out = []
    for k in range(8):
        ids = ids_ref[k : k + 1, :]
        slot = jnp.sum(jnp.where(ids == expert, ranks, 0.0), axis=0, keepdims=True)
        out.append(ids.astype(F32) * float(SLOTS) + slot)
    return jnp.concatenate(out + [comb_ref[...]], axis=0)


def kernel(
    q_ref, do_ref, k_ref, v_ref, mg_ref, ids_ref, comb_ref, w_ref,
    dq_ref, dk_ref, dv_ref, hid_ref,
    kv, tg, rows, snd, rcv, qs, dos, stat, dqt, dkv, xs1, xr1, xs2, xr2, zs, zr,
    ring_s, ring_r, kz_s, kz_r, tz_s, tz_r, xf_s, xf_r, xh_s, xh_r, xb_s, xb_r, xt_s, xt_r,
    a2a_s, a2a_r, core_s, core_r, r1_s, r1_r, r2_s, r2_r, rz_s, rz_r,
):
    y = lax.axis_index("dp")
    c = lax.axis_index("ctx")
    tp = lax.axis_index("tp")
    x, zl = c // NL, c % NL
    zh, core = tp // 2, tp % 2
    z = zh * NL + zl
    plane = y * NX + x

    def at(ax, ay, az, acore):
        return (ay, ax * NL + az % NL, (az // NL) * 2 + acore)

    z_up = at(x, y, (z + 1) % NZ, core)
    z_down = at(x, y, (z + NZ - 1) % NZ, core)
    x_up = at((x + 1) % NX, y, z, core)
    x_down = at((x + NX - 1) % NX, y, z, core)
    twin = at(x, y, z, 1 - core)

    def plane_dev(d):
        return at(d % NX, d // NX, z, core)

    def line_dev(j):
        return at(x, y, zh * NL + j, core)

    barrier = pltpu.get_barrier_semaphore()

    def greet(where):
        pl.semaphore_signal(barrier, inc=1, device_id=where, device_id_type=MESH)

    greet(z_up)
    greet(z_down)
    greet(twin)

    @pl.loop(1, 16)
    def _(i):
        greet(plane_dev((plane + i) % 16))

    @pl.loop(1, NL)
    def _(i):
        greet(line_dev((zl + i) % NL))

    kv[c, :, :HEAD_DIM] = k_ref[...]
    kv[c, :, HEAD_DIM:] = v_ref[...]
    rows[z] = mg_ref[...]
    tg[zl] = token_targets(ids_ref, comb_ref)
    for h in range(GROUP):
        qs[pl.ds(h * TOK, TOK), :] = q_ref[:, h * HEAD_DIM : (h + 1) * HEAD_DIM]
        dos[pl.ds(h * TOK, TOK), :] = do_ref[:, h * HEAD_DIM : (h + 1) * HEAD_DIM]
    pl.semaphore_wait(barrier, 3 + 15 + 7)

    half = (pl.ds(0, TOK // 2), pl.ds(TOK // 2, TOK // 2))

    def ring_copy(way, step, part, src):
        ref = rows.at[src, half[part]]
        return remote(
            ref, ref, (ring_s.at[way, part, step], ring_r.at[way, part, step]), (z_up, z_down)[way]
        )

    def kz_copy(way, step, src):
        ref = kv.at[x * NL + src]
        return remote(ref, ref, (kz_s.at[way, step], kz_r.at[way, step]), (z_up, z_down)[way])

    def tz_copy(way, step, src):
        ref = tg.at[src]
        return remote(ref, ref, (tz_s.at[way, step], tz_r.at[way, step]), (z_up, z_down)[way])

    def xf_copy(g, j):
        ref = kv.at[g * NL + j]
        return remote(ref, ref, (xf_s.at[j], xf_r.at[j]), x_up)

    def xh_copy(g, j):
        ref = kv.at[g * NL + j, half[0]]
        return remote(ref, ref, (xh_s.at[j], xh_r.at[j]), x_up)

    def xb_copy(part, g, j):
        ref = kv.at[g * NL + j, half[part]]
        return remote(ref, ref, (xb_s.at[part, j], xb_r.at[part, j]), x_down)

    def xt_copy(g, j):
        ref = kv.at[g * NL + j, half[1]]
        return remote(ref, ref, (xt_s.at[j], xt_r.at[j]), x_down)

    def x_send(j):
        @pl.when(x <= 2)
        def _():
            xf_copy(x, j).start()

        @pl.when(x == 0)
        def _():
            xb_copy(0, x, j).start()

        @pl.when(x <= 1)
        def _():
            xb_copy(1, x, j).start()

    x_send(zl)

    @pl.loop(0, NL)
    def _(s):
        up_src, down_src = zl - s, zl + s

        @pl.when((zl < NL - 1) & (up_src >= 0))
        def _():
            kz_copy(0, s, up_src).start()
            tz_copy(0, s, up_src).start()

        @pl.when((zl > 0) & (down_src < NL))
        def _():
            kz_copy(1, s, down_src).start()
            tz_copy(1, s, down_src).start()

        f_src, b_src = (z + NZ - s) % NZ, (z + s) % NZ
        ring_copy(0, s, 0, f_src).start()
        ring_copy(1, s, 1, b_src).start()

        @pl.when(s < NL - 1)
        def _():
            ring_copy(0, s, 1, f_src).start()
            ring_copy(1, s, 0, b_src).start()

        @pl.when(up_src >= 1)
        def _():
            kz_copy(0, s, up_src - 1).wait_recv()
            tz_copy(0, s, up_src - 1).wait_recv()
            x_send(up_src - 1)

        @pl.when(down_src < NL - 1)
        def _():
            kz_copy(1, s, down_src + 1).wait_recv()
            tz_copy(1, s, down_src + 1).wait_recv()
            x_send(down_src + 1)

        f_got, b_got = (z + NZ - s - 1) % NZ, (z + s + 1) % NZ
        ring_copy(0, s, 0, f_got).wait_recv()
        ring_copy(1, s, 1, b_got).wait_recv()

        @pl.when(s < NL - 1)
        def _():
            ring_copy(0, s, 1, f_got).wait_recv()
            ring_copy(1, s, 0, b_got).wait_recv()

    @pl.loop(0, NL)
    def _(j):
        @pl.when(x >= 1)
        def _():
            xf_copy(x - 1, j).wait_recv()

        @pl.when((x == 1) | (x == 2))
        def _():
            xh_copy(x - 1, j).start()

        @pl.when(x == 3)
        def _():
            xb_copy(0, 0, j).wait_recv()

        @pl.when((x == 3) | (x == 0))
        def _():
            g = (x + 1) % NX
            xb_copy(1, g, j).wait_recv()
            xt_copy(g, j).start()

    pick_row = lax.broadcasted_iota(jnp.int32, (16, TOK), 0)

    def send_copy(d):
        return remote(
            snd.at[d], rcv.at[core, plane], (a2a_s.at[d], a2a_r.at[plane]), plane_dev(d)
        )

    def got_copy(d):
        return remote(
            snd.at[d], rcv.at[core, d], (a2a_s.at[d], a2a_r.at[d]), plane_dev(d)
        )

    def twin_copy(d):
        return remote(
            rcv.at[core, d], rcv.at[core, d], (core_s.at[d], core_r.at[d]), twin
        )

    def twin_got(d):
        return remote(
            rcv.at[1 - core, d], rcv.at[1 - core, d], (core_s.at[d], core_r.at[d]), twin
        )

    @pl.loop(1, 17)
    def _(i):
        d = (plane + i) % 16
        expert = (d // NX) * (NX * NL) + (d % NX) * NL + zl
        columns = []
        for b in range(NL):
            first = (b * SLOTS) // 8 * 8
            place = pick_row + (first - b * SLOTS)
            inside = (place >= 0) & (place < SLOTS)
            key = jnp.where(inside, expert * SLOTS + place, -1).astype(F32)
            window = jnp.zeros((16, TOK), F32)
            for k in range(8):
                window += jnp.where(tg[b, k : k + 1, :] == key, tg[b, 8 + k : 9 + k, :], 0.0)
            pieces = [window]
            if first > 0:
                pieces = [jnp.zeros((first, TOK), F32)] + pieces
            if first + 16 < PACK:
                pieces = pieces + [jnp.zeros((PACK - first - 16, TOK), F32)]
            columns.append(jnp.concatenate(pieces, axis=0).astype(BF16))
        pick = jnp.concatenate(columns, axis=1)
        for part in range(2):
            source = rows[part * NL : (part + 1) * NL].reshape(RUN, 512)
            picked = dot_nn(pick, source).astype(BF16)
            snd[d, :, part * 512 : (part + 1) * 512] = picked

        @pl.when(i < 16)
        def _():
            send_copy(d).start()

    rcv[core, plane] = snd[plane]
    twin_copy(plane).start()

    @pl.when(x >= 2)
    def _():
        @pl.loop(0, NL)
        def _(j):
            xh_copy(x - 2, j).wait_recv()
            xt_copy(x - 2, j).wait_recv()

    lane = lax.broadcasted_iota(jnp.int32, (1, ROWS), 1)
    query_place = zl * TOK + lane % TOK

    def scores(g, i, masked):
        block = kv[pl.ds(g * NL + i * (CHUNK // TOK), CHUNK // TOK)].reshape(CHUNK, WIDE)
        keys, values = block[:, :HEAD_DIM], block[:, HEAD_DIM:]
        s = dot_nt(keys, qs[...]) * SCALE2
        if masked:
            place = i * CHUNK + lax.broadcasted_iota(jnp.int32, (CHUNK, ROWS), 0)
            s = jnp.where(place <= query_place, s, MASKED)
        return keys, s, dot_nt(values, dos[...])

    def stats_group(g, masked):
        @pl.loop(0, RUN // CHUNK)
        def _(i):
            _, s, dp = scores(g, i, masked)
            top = stat[0:1, :]
            new_top = jnp.maximum(top, jnp.max(s, axis=0, keepdims=True))
            e = jnp.exp2(s - new_top)
            shrink = jnp.exp2(top - new_top)
            stat[0:1, :] = new_top
            stat[1:2, :] = stat[1:2, :] * shrink + jnp.sum(e, axis=0, keepdims=True)
            stat[2:3, :] = stat[2:3, :] * shrink + jnp.sum(e * dp, axis=0, keepdims=True)

    stat[0:1, :] = jnp.full((1, ROWS), MASKED, F32)
    stat[1:3, :] = jnp.zeros((2, ROWS), F32)
    stats_group(x, True)

    @pl.loop(0, x)
    def _(g):
        stats_group(g, False)

    stat[2:3, :] = stat[2:3, :] / stat[1:2, :]
    stat[0:1, :] = stat[0:1, :] + jnp.log2(stat[1:2, :])
    dqt[...] = jnp.zeros_like(dqt)

    def grads_group(g, masked):
        @pl.loop(0, RUN // CHUNK)
        def _(i):
            keys, s, dp = scores(g, i, masked)
            p = jnp.exp2(s - stat[0:1, :])
            ds = (p * (dp - stat[2:3, :])).astype(BF16)
            here = pl.ds(pl.multiple_of(i * CHUNK, CHUNK), CHUNK)
            dkv[g, here, HEAD_DIM:] = dot_nn(p.astype(BF16), dos[...])
            dkv[g, here, :HEAD_DIM] = dot_nn(ds, qs[...])
            dqt[...] += dot_tn(keys, ds)

    def r1_copy(way):
        return remote(
            xs1.at[way], xr1.at[way], (r1_s.at[way], r1_r.at[way]), (x_up, x_down)[way]
        )

    def r2_copy(way, part, src=None):
        ref = xs2.at[way, part] if src is None else src
        return remote(
            ref, xr2.at[way, part], (r2_s.at[way, part], r2_r.at[way, part]), (x_up, x_down)[way]
        )

    first, second = pl.ds(0, RUN // 2), pl.ds(RUN // 2, RUN // 2)

    @pl.when(x >= 2)
    def _():
        grads_group(x - 2, False)
        xs1[0] = dkv[x - 2, first, :].astype(BF16)
        xs1[1] = dkv[x - 2, second, :].astype(BF16)
        r1_copy(0).start()
        r1_copy(1).start()

    @pl.when(x == 3)
    def _():
        grads_group(0, False)

    @pl.when(x >= 1)
    def _():
        grads_group(x - 1, False)
        xs2[1, 0] = dkv[x - 1, first, :].astype(BF16)
        r2_copy(1, 0).start()

    @pl.when(x == 3)
    def _():
        xs2[0, 1] = dkv[0, second, :].astype(BF16)
        r2_copy(0, 1).start()
        xs2[1, 1] = dkv[2, second, :].astype(BF16)
        r2_copy(1, 1).start()
        r1_copy(0).wait_recv()
        xs2[0, 0] = (dkv[0, first, :] + xr1[0].astype(F32)).astype(BF16)
        r2_copy(0, 0).start()

    @pl.when((x == 1) | (x == 2))
    def _():
        r1_copy(1).wait_recv()
        xs2[1, 1] = (dkv[x - 1, second, :] + xr1[1].astype(F32)).astype(BF16)
        r2_copy(1, 1).start()

    @pl.when(x == 0)
    def _():
        r1_copy(0).wait_recv()
        r2_copy(0, 0, xr1.at[0]).start()

    grads_group(x, True)
    for h in range(GROUP):
        here = slice(h * TOK, (h + 1) * TOK)
        dq_ref[:, here] = (dqt[:, here].T * SCALE).astype(BF16)

    @pl.loop(1, 16)
    def _(i):
        d = (plane + 16 - i) % 16
        got_copy(d).wait_recv()
        twin_copy(d).start()

    @pl.when(x <= 2)
    def _():
        r2_copy(1, 0).wait_recv()
        dkv[x, first, :] += xr2[1, 0].astype(F32)
        r2_copy(1, 1).wait_recv()
        dkv[x, second, :] += xr2[1, 1].astype(F32)

    @pl.when(x <= 1)
    def _():
        r2_copy(0, 0).wait_recv()
        dkv[x, first, :] += xr2[0, 0].astype(F32)

    @pl.when(x == 0)
    def _():
        r2_copy(0, 1).wait_recv()
        dkv[x, second, :] += xr2[0, 1].astype(F32)

    def rz_send(j):
        return remote(zs.at[j], zr.at[zl], (rz_s.at[j], rz_r.at[zl]), line_dev(j))

    def rz_got(j):
        return remote(zs.at[j], zr.at[j], (rz_s.at[j], rz_r.at[j]), line_dev(j))

    @pl.loop(1, NL)
    def _(i):
        j = (zl + i) % NL
        zs[j] = dkv[x, pl.ds(pl.multiple_of(j * TOK, TOK), TOK), :].astype(BF16)
        rz_send(j).start()

    twin_got(plane).wait_recv()

    @pl.loop(1, 16)
    def _(i):
        twin_got((plane + 16 - i) % 16).wait_recv()

    @pl.loop(0, 4)
    def _(i):
        total = jnp.zeros((4 * PACK, w_ref.shape[0]), F32)
        for side in range(2):
            for part in range(2):
                at_feature = (part * 2 + side) * 512
                left = rcv[side, pl.ds(i * 4, 4), :, part * 512 : (part + 1) * 512]
                total += dot_nt(
                    left.reshape(4 * PACK, 512), w_ref[:, at_feature : at_feature + 512]
                )
        for b in range(4 * NL):
            hid_ref[i * (4 * NL) + b] = total[b * SLOTS : (b + 1) * SLOTS, :].astype(BF16)

    @pl.loop(1, NL)
    def _(i):
        j = (zl + i) % NL
        rz_got(j).wait_recv()
        dkv[x, pl.ds(pl.multiple_of(zl * TOK, TOK), TOK), :] += zr[j].astype(F32)

    own = dkv[x, pl.ds(pl.multiple_of(zl * TOK, TOK), TOK), :]
    dk_ref[...] = (own[:, :HEAD_DIM] * SCALE).astype(BF16)
    dv_ref[...] = own[:, HEAD_DIM:].astype(BF16)

    @pl.loop(0, NL)
    def _(s):
        @pl.when((zl < NL - 1) & (zl - s >= 0))
        def _():
            kz_copy(0, s, zl - s).wait_send()
            tz_copy(0, s, zl - s).wait_send()

        @pl.when((zl > 0) & (zl + s < NL))
        def _():
            kz_copy(1, s, zl + s).wait_send()
            tz_copy(1, s, zl + s).wait_send()

        ring_copy(0, s, 0, (z + NZ - s) % NZ).wait_send()
        ring_copy(1, s, 1, (z + s) % NZ).wait_send()

        @pl.when(s < NL - 1)
        def _():
            ring_copy(0, s, 1, (z + NZ - s) % NZ).wait_send()
            ring_copy(1, s, 0, (z + s) % NZ).wait_send()

        @pl.when(x <= 2)
        def _():
            xf_copy(x, s).wait_send()

        @pl.when(x == 0)
        def _():
            xb_copy(0, x, s).wait_send()

        @pl.when(x <= 1)
        def _():
            xb_copy(1, x, s).wait_send()

        @pl.when((x == 1) | (x == 2))
        def _():
            xh_copy(x - 1, s).wait_send()

        @pl.when((x == 3) | (x == 0))
        def _():
            xt_copy((x + 1) % NX, s).wait_send()

    twin_copy(plane).wait_send()

    @pl.loop(1, 16)
    def _(i):
        d = (plane + i) % 16
        send_copy(d).wait_send()
        twin_copy(d).wait_send()

    @pl.when(x >= 2)
    def _():
        r1_copy(0).wait_send()
        r1_copy(1).wait_send()

    @pl.when(x >= 1)
    def _():
        r2_copy(1, 0).wait_send()
        r2_copy(1, 1).wait_send()

    @pl.when((x == 3) | (x == 0))
    def _():
        r2_copy(0, 0).wait_send()

    @pl.when(x == 3)
    def _():
        r2_copy(0, 1).wait_send()

    @pl.loop(1, NL)
    def _(i):
        rz_send((zl + i) % NL).wait_send()


def per_device(queries, keys, values, out_grad, mixed_grad, expert_ids, combine, w_down):
    ids = expert_ids.T
    weights = combine.T.astype(F32)
    vmem = pl.BlockSpec(memory_space=pltpu.VMEM)
    dma = pltpu.SemaphoreType.DMA
    hid = w_down.shape[1]
    shapes = (
        jax.ShapeDtypeStruct((TOK, ROWS), BF16),
        jax.ShapeDtypeStruct((TOK, HEAD_DIM), BF16),
        jax.ShapeDtypeStruct((TOK, HEAD_DIM), BF16),
        jax.ShapeDtypeStruct((EXPERTS, SLOTS, hid), BF16),
    )
    scratch = [
        pltpu.VMEM((NX * NL, TOK, WIDE), BF16),
        pltpu.VMEM((NL, 16, TOK), F32),
        pltpu.VMEM((NZ, TOK, 512), BF16),
        pltpu.VMEM((16, PACK, 1024), BF16),
        pltpu.VMEM((2, 16, PACK, 1024), BF16),
        pltpu.VMEM((ROWS, HEAD_DIM), BF16),
        pltpu.VMEM((ROWS, HEAD_DIM), BF16),
        pltpu.VMEM((8, ROWS), F32),
        pltpu.VMEM((HEAD_DIM, ROWS), F32),
        pltpu.VMEM((NX, RUN, WIDE), F32),
        pltpu.VMEM((2, RUN // 2, WIDE), BF16),
        pltpu.VMEM((2, RUN // 2, WIDE), BF16),
        pltpu.VMEM((2, 2, RUN // 2, WIDE), BF16),
        pltpu.VMEM((2, 2, RUN // 2, WIDE), BF16),
        pltpu.VMEM((NL, TOK, WIDE), BF16),
        pltpu.VMEM((NL, TOK, WIDE), BF16),
    ]
    for shape in (
        (2, 2, NL), (2, NL), (2, NL), (NL,), (NL,), (2, NL), (NL,),
        (16,), (16,), (2,), (2, 2), (NL,),
    ):
        scratch += [dma(shape), dma(shape)]
    dq, dk, dv, hidden = pl.pallas_call(
        kernel,
        out_shape=shapes,
        in_specs=[vmem] * 8,
        out_specs=(vmem,) * 4,
        scratch_shapes=scratch,
        compiler_params=pltpu.CompilerParams(
            collective_id=0, has_side_effects=True, vmem_limit_bytes=56 * 1024 * 1024
        ),
        name="layer_backward",
    )(queries[0], out_grad[0], keys[0], values[0], mixed_grad, ids, weights, w_down[0])
    return dq[None], dk[None], dv[None], hidden[None]


def solution(mesh):
    placed = (
        P("dp", "ctx", "tp"),
        P("dp", "ctx", "tp"),
        P("dp", "ctx", "tp"),
        P("dp", "ctx", "tp"),
        P(("dp", "ctx"), "tp"),
        P(("dp", "ctx"), None),
        P(("dp", "ctx"), None),
        P(("dp", "ctx"), "tp", None),
    )
    return jax.shard_map(
        per_device,
        mesh=mesh,
        in_specs=placed,
        out_specs=(
            P("dp", "ctx", "tp"),
            P("dp", "ctx", "tp"),
            P("dp", "ctx", "tp"),
            P(("dp", "ctx"), None, None, "tp"),
        ),
        check_vma=False,
    )
```

```python
import functools
import math

import jax
import jax.numpy as jnp
from jax import lax
from jax.experimental import pallas as pl
from jax.experimental.pallas import tpu as pltpu
from jax.sharding import PartitionSpec as P

MESH = pl.DeviceIdType.MESH
HEAD_DIM = 128
GROUP = 8
TOK = 128
SLOTS = 10
EXPERTS = 128
NX, NY, NL, NZ = 4, 4, 8, 16
RUN = NL * TOK
WIDE = 2 * HEAD_DIM
CHUNK = 256
ROWS = GROUP * TOK
PACK = NL * SLOTS
SIDE = 16
PART = 512
SCALE = HEAD_DIM**-0.5
SCALE2 = SCALE / math.log(2.0)
MASKED = -1e30
F32, BF16 = jnp.float32, jnp.bfloat16


def dot_nt(a, b):
    return lax.dot_general(a, b, (((1,), (1,)), ((), ())), preferred_element_type=F32)


def dot_nn(a, b):
    return lax.dot_general(a, b, (((1,), (0,)), ((), ())), preferred_element_type=F32)


def dot_tn(a, b):
    return lax.dot_general(a, b, (((0,), (0,)), ((), ())), preferred_element_type=F32)


def remote(src, dst, sems, where):
    return pltpu.make_async_remote_copy(
        src_ref=src,
        dst_ref=dst,
        send_sem=sems[0],
        recv_sem=sems[1],
        device_id=where,
        device_id_type=MESH,
    )


def token_targets(ids, weights):
    expert = lax.broadcasted_iota(jnp.int32, (EXPERTS, TOK), 0).astype(F32)
    hits = jnp.zeros((EXPERTS, TOK), F32)
    for k in range(8):
        hits += jnp.where(ids[k : k + 1, :] == expert, 1.0, 0.0)
    rows = lax.broadcasted_iota(jnp.int32, (TOK, TOK), 0)
    cols = lax.broadcasted_iota(jnp.int32, (TOK, TOK), 1)
    before = jnp.where(rows < cols, 1.0, 0.0).astype(BF16)
    ranks = dot_nn(hits.astype(BF16), before)
    slots = [
        jnp.sum(jnp.where(ids[k : k + 1, :] == expert, ranks, 0.0), axis=0, keepdims=True)
        for k in range(8)
    ]
    slots = jnp.concatenate(slots, axis=0)
    top = jnp.concatenate([ids, slots, weights, jnp.zeros_like(ids)], axis=1)
    return jnp.concatenate([top, jnp.zeros_like(top)], axis=0).astype(BF16)


def kernel(
    q_ref, do_ref, k_ref, v_ref, mg_ref, ids_ref, comb_ref, w_ref,
    dq_ref, dk_ref, dv_ref, hid_ref,
    kv, rows, picks, snd, rcv, qs, dos, stat, dqt, dkv, xs1, xr1, xs2, xr2, zs, zr,
    ring_s, ring_r, kz_s, kz_r, xf_s, xf_r, xh_s, xh_r, xb_s, xb_r, xt_s, xt_r,
    a2a_s, a2a_r, all_s, all_r, core_s, core_r, r1_s, r1_r, r2_s, r2_r, rz_s, rz_r,
):
    y = lax.axis_index("dp")
    c = lax.axis_index("ctx")
    tp = lax.axis_index("tp")
    x, zl = c // NL, c % NL
    zh, core = tp // 2, tp % 2
    z = zh * NL + zl
    plane = y * NX + x

    def at(ax, ay, az, acore):
        return (ay, ax * NL + az % NL, (az // NL) * 2 + acore)

    z_up = at(x, y, (z + 1) % NZ, core)
    z_down = at(x, y, (z + NZ - 1) % NZ, core)
    x_up = at((x + 1) % NX, y, z, core)
    x_down = at((x + NX - 1) % NX, y, z, core)
    twin = at(x, y, z, 1 - core)

    def plane_dev(d):
        return at(d % NX, d // NX, z, core)

    def line_dev(j):
        return at(x, y, zh * NL + j, core)

    barrier = pltpu.get_barrier_semaphore()

    def greet(where):
        pl.semaphore_signal(barrier, inc=1, device_id=where, device_id_type=MESH)

    greet(z_up)
    greet(z_down)
    greet(twin)

    @pl.loop(1, 16)
    def _(i):
        greet(plane_dev((plane + i) % 16))

    @pl.loop(1, NL)
    def _(i):
        greet(line_dev((zl + i) % NL))

    kv[c, :, :HEAD_DIM] = k_ref[...]
    kv[c, :, HEAD_DIM:] = v_ref[...]
    rows[8, pl.ds(SIDE, TOK), :] = mg_ref[...]
    rows[8, pl.ds(0, SIDE), :] = token_targets(
        ids_ref[...].astype(F32), comb_ref[...].astype(F32)
    )
    for h in range(GROUP):
        qs[pl.ds(h * TOK, TOK), :] = q_ref[:, h * HEAD_DIM : (h + 1) * HEAD_DIM]
        dos[pl.ds(h * TOK, TOK), :] = do_ref[:, h * HEAD_DIM : (h + 1) * HEAD_DIM]
    stat[0:1, :] = jnp.full((1, ROWS), MASKED, F32)
    stat[1:3, :] = jnp.zeros((2, ROWS), F32)
    pl.semaphore_wait(barrier, 3 + 15 + 7)

    half = (pl.ds(0, TOK // 2), pl.ds(TOK // 2, TOK // 2))
    whole = pl.ds(0, SIDE + TOK // 2)
    piece = (pl.ds(SIDE, TOK // 2), pl.ds(SIDE + TOK // 2, TOK // 2))

    def ring(way, part, s, op):
        near = (8 - s, 8 + s)[way]
        far = (7 - s, (9 + s) % NZ)[way]
        last = (3, 2)[way]

        def copy(span):
            if op != "wait_recv":
                source, target = rows.at[near, span], rows.at[far, span]
            else:
                source, target = rows.at[far, span], rows.at[far, span]
            sems = (ring_s.at[way, part, s], ring_r.at[way, part, s])
            getattr(remote(source, target, sems, (z_up, z_down)[way]), op)()

        if part == 1:
            copy(piece[1])
        else:
            pl.when(s <= last)(lambda: copy(whole))
            pl.when(s > last)(lambda: copy(piece[0]))

    def kz_copy(way, step, src):
        ref = kv.at[x * NL + src]
        return remote(ref, ref, (kz_s.at[way, step], kz_r.at[way, step]), (z_up, z_down)[way])

    def xf_copy(g, j):
        ref = kv.at[g * NL + j]
        return remote(ref, ref, (xf_s.at[j], xf_r.at[j]), x_up)

    def xh_copy(g, j):
        ref = kv.at[g * NL + j, half[0]]
        return remote(ref, ref, (xh_s.at[j], xh_r.at[j]), x_up)

    def xb_copy(part, g, j):
        ref = kv.at[g * NL + j, half[part]]
        return remote(ref, ref, (xb_s.at[part, j], xb_r.at[part, j]), x_down)

    def xt_copy(g, j):
        ref = kv.at[g * NL + j, half[1]]
        return remote(ref, ref, (xt_s.at[j], xt_r.at[j]), x_down)

    def x_send(j):
        @pl.when(x <= 2)
        def _():
            xf_copy(x, j).start()

        @pl.when(x == 0)
        def _():
            xb_copy(0, x, j).start()

        @pl.when(x <= 1)
        def _():
            xb_copy(1, x, j).start()

    lane = lax.broadcasted_iota(jnp.int32, (1, ROWS), 1) % TOK

    def scores(slot, count, first):
        size = count * TOK
        block = kv[pl.ds(slot, count)].reshape(size, WIDE)
        keys, values = block[:, :HEAD_DIM], block[:, HEAD_DIM:]
        s = dot_nt(keys, qs[...]) * SCALE2
        if first is not None:
            place = lax.broadcasted_iota(jnp.int32, (size, ROWS), 0)
            s = jnp.where(place <= lane + first, s, MASKED)
        return keys, s, dot_nt(values, dos[...])

    def stats(slot, count, first=None):
        _, s, dp = scores(slot, count, first)
        top = stat[0:1, :]
        new_top = jnp.maximum(top, jnp.max(s, axis=0, keepdims=True))
        e = jnp.exp2(s - new_top)
        shrink = jnp.exp2(top - new_top)
        stat[0:1, :] = new_top
        stat[1:2, :] = stat[1:2, :] * shrink + jnp.sum(e, axis=0, keepdims=True)
        stat[2:3, :] = stat[2:3, :] * shrink + jnp.sum(e * dp, axis=0, keepdims=True)

    def x_pass(j):
        @pl.when((j >= 0) & (j < NL))
        def _():
            @pl.when(x >= 1)
            def _():
                xf_copy(x - 1, j).wait_recv()

            @pl.when((x == 1) | (x == 2))
            def _():
                xh_copy(x - 1, j).start()

            @pl.when(x == 3)
            def _():
                xb_copy(0, 0, j).wait_recv()

            @pl.when((x == 3) | (x == 0))
            def _():
                xb_copy(1, (x + 1) % NX, j).wait_recv()
                xt_copy((x + 1) % NX, j).start()

            @pl.when(x >= 1)
            def _():
                stats((x - 1) * NL + j, 1)

            @pl.when(x == 3)
            def _():
                stats(j, 1)

    pick_row = lax.broadcasted_iota(jnp.int32, (16, TOK), 0)
    pick_block = lax.broadcasted_iota(jnp.int32, (NL, TOK), 0)

    def make_pick(r):
        d = (plane + r + 1) % 16
        expert = (d // NX) * (NX * NL) + (d % NX) * NL + zl
        key = jnp.where(pick_row < SLOTS, expert * SLOTS + pick_row, -1).astype(F32)
        columns = []
        for n in range(NL):
            named = rows[4 + n, pl.ds(0, SIDE), :].astype(F32)
            target = named[:8, :TOK] * float(SLOTS) + named[:8, TOK : 2 * TOK]
            weight = named[:8, 2 * TOK : 3 * TOK]
            window = jnp.zeros((16, TOK), F32)
            for k in range(8):
                window += jnp.where(target[k : k + 1, :] == key, weight[k : k + 1, :], 0.0)
            mine = pick_block == (zl + 4 + n) % NL
            column = [jnp.where(mine, window[i : i + 1, :], 0.0) for i in range(SLOTS)]
            columns.append(jnp.concatenate(column, axis=0).astype(BF16))
        picks[r] = jnp.concatenate(columns, axis=1)

    def a2a_out(w, r):
        return remote(
            snd.at[w, r], rcv.at[core, w, plane], (a2a_s.at[w, r], a2a_r.at[w, plane]),
            plane_dev((plane + r + 1) % 16),
        )

    def a2a_in(w, d):
        return remote(
            snd.at[w, 0], rcv.at[core, w, d], (a2a_s.at[w, 0], a2a_r.at[w, d]), plane_dev(d)
        )

    def pack_rows(w, n):
        if w == 0:
            @pl.loop(0, 4)
            def _(i):
                make_pick(n * 4 + i)

        total = jnp.zeros((4 * PACK, PART), F32)
        for m, start in enumerate(((4, 8), (12, 0))[w]):
            source = rows[start : start + 4, SIDE:, :].reshape(4 * TOK, PART)
            chosen = picks[pl.ds(n * 4, 4), :, m * 4 * TOK : (m + 1) * 4 * TOK]
            total += dot_nn(chosen.reshape(4 * PACK, 4 * TOK), source)
        snd[w, pl.ds(n * 4, 4)] = total.astype(BF16).reshape(4, PACK, PART)

        @pl.when(n == 3)
        def _():
            rcv[core, w, plane] = snd[w, 15]

    def launch_rows(w, n):
        @pl.loop(0, 4)
        def _(i):
            r = n * 4 + i

            @pl.when(r < 15)
            def _():
                a2a_out(w, r).start()

    @pl.when(zl < NL - 1)
    def _():
        kz_copy(0, 0, zl).start()

    @pl.when(zl > 0)
    def _():
        kz_copy(1, 0, zl).start()

    x_send(zl)
    ring(0, 0, 0, "start")
    ring(1, 1, 0, "start")
    ring(0, 1, 0, "start")
    ring(1, 0, 0, "start")
    stats(c, 1, 0)

    @pl.loop(0, NL + 1)
    def _(s):
        below, above = zl - 1 - s, zl + 1 + s

        @pl.when(below >= 0)
        def _():
            kz_copy(0, s, below).wait_recv()

            @pl.when(zl < NL - 1)
            def _():
                kz_copy(0, s + 1, below).start()

        @pl.when(above < NL)
        def _():
            kz_copy(1, s, above).wait_recv()

            @pl.when(zl > 0)
            def _():
                kz_copy(1, s + 1, above).start()

        @pl.when(below >= 0)
        def _():
            x_send(below)

        @pl.when(above < NL)
        def _():
            x_send(above)

        @pl.when(below >= 0)
        def _():
            stats(x * NL + below, 1)

        for way, part in ((0, 0), (1, 1), (0, 1), (1, 0)):
            most = NL if way == part else NL - 1

            @pl.when((s >= 1) & (s <= most))
            def _():
                ring(way, part, s - 1, "wait_recv")

                @pl.when(s < most)
                def _():
                    ring(way, part, s, "start")

        @pl.when(s == 1)
        def _():
            x_pass(zl)

        @pl.when(s >= 2)
        def _():
            x_pass(zl + 1 - s)
            x_pass(zl - 1 + s)

        @pl.when(s >= 5)
        def _():
            pack_rows(0, s - 5)

            launch_rows(0, s - 5)

    @pl.when(x == 0)
    def _():
        @pl.loop(0, 4)
        def _(n):
            pack_rows(1, n)
            launch_rows(1, n)

    @pl.when(x >= 2)
    def _():
        @pl.loop(0, NL)
        def _(j):
            xh_copy(x - 2, j).wait_recv()
            xt_copy(x - 2, j).wait_recv()

        @pl.loop(0, 2)
        def _(i):
            stats((x - 2) * NL + i * 4, 4)

    stat[2:3, :] = stat[2:3, :] / stat[1:2, :]
    stat[0:1, :] = stat[0:1, :] + jnp.log2(stat[1:2, :])
    dqt[...] = jnp.zeros_like(dqt)
    def span(part):
        return pl.ds(pl.multiple_of(part * CHUNK, CHUNK), CHUNK)

    def grads(g, part, masked=False):
        first = (zl - part * 2) * TOK if masked else None
        keys, s, dp = scores(g * NL + part * 2, 2, first)
        p = jnp.exp2(s - stat[0:1, :])
        ds = (p * (dp - stat[2:3, :])).astype(BF16)
        dkv[g, span(part), HEAD_DIM:] = dot_nn(p.astype(BF16), dos[...])
        dkv[g, span(part), :HEAD_DIM] = dot_nn(ds, qs[...])
        dqt[...] += dot_tn(keys, ds)

    def r1_copy(way, part):
        return remote(
            xs1.at[part], xr1.at[part], (r1_s.at[part], r1_r.at[part]), (x_up, x_down)[way]
        )

    def r2_copy(way, part, src=None):
        ref = xs2.at[way, part] if src is None else src
        return remote(
            ref, xr2.at[way, part], (r2_s.at[way, part], r2_r.at[way, part]), (x_up, x_down)[way]
        )

    def rz_send(j):
        return remote(zs.at[j], zr.at[zl], (rz_s.at[j], rz_r.at[zl]), line_dev(j))

    def rz_got(j):
        return remote(zs.at[j], zr.at[j], (rz_s.at[j], rz_r.at[j]), line_dev(j))

    def z_spread(part):
        @pl.loop(0, 2)
        def _(i):
            j = part * 2 + (zl + i) % 2

            @pl.when(j != zl)
            def _():
                zs[j] = dkv[x, pl.ds(pl.multiple_of(j * TOK, TOK), TOK), :].astype(BF16)
                rz_send(j).start()

    @pl.when(x >= 2)
    def _():
        @pl.loop(0, 4)
        def _(part):
            grads(x - 2, part)
            xs1[part] = dkv[x - 2, span(part), :].astype(BF16)
            pl.when(part < 2)(lambda: r1_copy(0, part).start())
            pl.when(part >= 2)(lambda: r1_copy(1, part).start())

    @pl.when(x == 3)
    def _():
        @pl.loop(0, 4)
        def _(n):
            part = (n + 2) % 4
            grads(0, part)

            @pl.when(part < 2)
            def _():
                r1_copy(0, part).wait_recv()
                dkv[0, span(part), :] += xr1[part].astype(F32)

            xs2[0, part] = dkv[0, span(part), :].astype(BF16)
            r2_copy(0, part).start()

    @pl.when(x >= 1)
    def _():
        @pl.loop(0, 4)
        def _(part):
            grads(x - 1, part)

            @pl.when((part >= 2) & (x < 3))
            def _():
                r1_copy(1, part).wait_recv()
                dkv[x - 1, span(part), :] += xr1[part].astype(F32)

            xs2[1, part] = dkv[x - 1, span(part), :].astype(BF16)
            r2_copy(1, part).start()

    @pl.loop(0, 4)
    def _(part):
        grads(x, part, True)
        pl.when(x == 3)(lambda: z_spread(part))

    @pl.when(x >= 1)
    def _():
        @pl.loop(0, 4)
        def _(n):
            pack_rows(1, n)
            launch_rows(1, n)

    @pl.when(x == 0)
    def _():
        @pl.loop(0, 2)
        def _(part):
            r1_copy(0, part).wait_recv()
            r2_copy(0, part, xr1.at[part]).start()

    for h in range(GROUP):
        at_head = slice(h * TOK, (h + 1) * TOK)
        dq_ref[:, at_head] = (dqt[:, at_head].T * SCALE).astype(BF16)

    def all_copy(side):
        ref = rcv.at[side, 0]
        return remote(ref, ref, (all_s, all_r), twin)

    def core_copy(side, d):
        ref = rcv.at[side, 1, d]
        return remote(ref, ref, (core_s.at[d], core_r.at[d]), twin)

    @pl.loop(1, 16)
    def _(i):
        a2a_in(0, (plane + 16 - i) % 16).wait_recv()

    all_copy(core).start()

    @pl.loop(0, 4)
    def _(part):
        @pl.when(x <= 2)
        def _():
            r2_copy(1, part).wait_recv()
            dkv[x, span(part), :] += xr2[1, part].astype(F32)

            @pl.when((x == 0) | ((x == 1) & (part < 2)))
            def _():
                r2_copy(0, part).wait_recv()
                dkv[x, span(part), :] += xr2[0, part].astype(F32)

            z_spread(part)

    core_copy(core, plane).start()

    @pl.loop(1, 16)
    def _(i):
        d = (plane + 16 - i) % 16
        a2a_in(1, d).wait_recv()
        core_copy(core, d).start()

    all_copy(1 - core).wait_recv()

    @pl.loop(0, 16)
    def _(i):
        core_copy(1 - core, (plane + 16 - i) % 16).wait_recv()

    block = lax.broadcasted_iota(jnp.int32, (4 * PACK, PART), 0) % NL
    low = (z + 12 + (block + 12 - zl) % NL) % NZ < NL

    @pl.loop(0, 4)
    def _(i):
        total = jnp.zeros((4 * PACK, w_ref.shape[0]), F32)
        for side in range(2):
            near = rcv[side, 0, pl.ds(i * 4, 4)].reshape(4 * PACK, PART)
            far = rcv[side, 1, pl.ds(i * 4, 4)].reshape(4 * PACK, PART)
            for part in range(2):
                left = jnp.where(low, near, far) if part == 0 else jnp.where(low, far, near)
                begin = (part * 2 + side) * PART
                total += dot_nt(left, w_ref[:, begin : begin + PART])
        for n in range(SLOTS):
            parts = [total[m * PACK + n * NL : m * PACK + (n + 1) * NL, :] for m in range(4)]
            here = pl.ds(pl.multiple_of(i * 4 * NL, 4 * NL), 4 * NL)
            hid_ref[n, here, :] = jnp.concatenate(parts, axis=0).astype(BF16)

    mine = pl.ds(pl.multiple_of(zl * TOK, TOK), TOK)

    @pl.loop(1, NL)
    def _(i):
        j = (zl + i) % NL
        rz_got(j).wait_recv()
        dkv[x, mine, :] += zr[j].astype(F32)

    own = dkv[x, mine, :]
    dk_ref[...] = (own[:, :HEAD_DIM] * SCALE).astype(BF16)
    dv_ref[...] = own[:, HEAD_DIM:].astype(BF16)

    @pl.loop(0, NL)
    def _(s):
        @pl.when((zl < NL - 1) & (zl - s >= 0))
        def _():
            kz_copy(0, s, zl - s).wait_send()

        @pl.when((zl > 0) & (zl + s < NL))
        def _():
            kz_copy(1, s, zl + s).wait_send()

        ring(0, 0, s, "wait_send")
        ring(1, 1, s, "wait_send")

        @pl.when(s < NL - 1)
        def _():
            ring(0, 1, s, "wait_send")
            ring(1, 0, s, "wait_send")

        @pl.when(x <= 2)
        def _():
            xf_copy(x, s).wait_send()

        @pl.when(x == 0)
        def _():
            xb_copy(0, x, s).wait_send()

        @pl.when(x <= 1)
        def _():
            xb_copy(1, x, s).wait_send()

        @pl.when((x == 1) | (x == 2))
        def _():
            xh_copy(x - 1, s).wait_send()

        @pl.when((x == 3) | (x == 0))
        def _():
            xt_copy((x + 1) % NX, s).wait_send()

    all_copy(core).wait_send()
    core_copy(core, plane).wait_send()

    @pl.loop(0, 15)
    def _(r):
        a2a_out(0, r).wait_send()
        a2a_out(1, r).wait_send()
        core_copy(core, (plane + r + 1) % 16).wait_send()

    @pl.loop(0, 4)
    def _(part):
        @pl.when(x >= 2)
        def _():
            pl.when(part < 2)(lambda: r1_copy(0, part).wait_send())
            pl.when(part >= 2)(lambda: r1_copy(1, part).wait_send())

        @pl.when(x >= 1)
        def _():
            r2_copy(1, part).wait_send()

        @pl.when((x == 3) | ((x == 0) & (part < 2)))
        def _():
            r2_copy(0, part).wait_send()

    @pl.loop(1, NL)
    def _(i):
        rz_send((zl + i) % NL).wait_send()


def per_device(queries, keys, values, out_grad, mixed_grad, expert_ids, combine, w_down):
    vmem = pl.BlockSpec(memory_space=pltpu.VMEM)
    dma = pltpu.SemaphoreType.DMA
    hid = w_down.shape[1]
    shapes = (
        jax.ShapeDtypeStruct((TOK, ROWS), BF16),
        jax.ShapeDtypeStruct((TOK, HEAD_DIM), BF16),
        jax.ShapeDtypeStruct((TOK, HEAD_DIM), BF16),
        jax.ShapeDtypeStruct((SLOTS, EXPERTS, hid), BF16),
    )
    scratch = [
        pltpu.VMEM((NX * NL, TOK, WIDE), BF16),
        pltpu.VMEM((NZ, SIDE + TOK, PART), BF16),
        pltpu.VMEM((16, PACK, RUN), BF16),
        pltpu.VMEM((2, 16, PACK, PART), BF16),
        pltpu.VMEM((2, 2, 16, PACK, PART), BF16),
        pltpu.VMEM((ROWS, HEAD_DIM), BF16),
        pltpu.VMEM((ROWS, HEAD_DIM), BF16),
        pltpu.VMEM((8, ROWS), F32),
        pltpu.VMEM((HEAD_DIM, ROWS), F32),
        pltpu.VMEM((NX, RUN, WIDE), F32),
        pltpu.VMEM((4, CHUNK, WIDE), BF16),
        pltpu.VMEM((4, CHUNK, WIDE), BF16),
        pltpu.VMEM((2, 4, CHUNK, WIDE), BF16),
        pltpu.VMEM((2, 4, CHUNK, WIDE), BF16),
        pltpu.VMEM((NL, TOK, WIDE), BF16),
        pltpu.VMEM((NL, TOK, WIDE), BF16),
    ]
    for shape in (
        (2, 2, NL), (2, NL), (NL,), (NL,), (2, NL), (NL,),
        (2, 16), (), (16,), (4,), (2, 4), (NL,),
    ):
        scratch += [dma(shape), dma(shape)]
    dq, dk, dv, hidden = pl.pallas_call(
        kernel,
        out_shape=shapes,
        in_specs=[vmem] * 8,
        out_specs=(vmem,) * 4,
        scratch_shapes=scratch,
        compiler_params=pltpu.CompilerParams(
            collective_id=0, has_side_effects=True, vmem_limit_bytes=56 * 1024 * 1024
        ),
        name="layer_backward",
    )(queries[0], out_grad[0], keys[0], values[0], mixed_grad, expert_ids.T, combine.T, w_down[0])
    return dq[None], dk[None], dv[None], hidden.transpose(1, 0, 2)[None]


def solution(mesh):
    placed = (
        P("dp", "ctx", "tp"),
        P("dp", "ctx", "tp"),
        P("dp", "ctx", "tp"),
        P("dp", "ctx", "tp"),
        P(("dp", "ctx"), "tp"),
        P(("dp", "ctx"), None),
        P(("dp", "ctx"), None),
        P(("dp", "ctx"), "tp", None),
    )
    return jax.shard_map(
        per_device,
        mesh=mesh,
        in_specs=placed,
        out_specs=(
            P("dp", "ctx", "tp"),
            P("dp", "ctx", "tp"),
            P("dp", "ctx", "tp"),
            P(("dp", "ctx"), None, None, "tp"),
        ),
        check_vma=False,
    )
```

```python
import functools
import math

import jax
import jax.numpy as jnp
from jax import lax
from jax.experimental import pallas as pl
from jax.experimental.pallas import tpu as pltpu
from jax.sharding import PartitionSpec as P

MESH = pl.DeviceIdType.MESH
HEAD_DIM = 128
GROUP = 8
TOK = 128
SLOTS = 10
EXPERTS = 128
NX, NY, NL, NZ = 4, 4, 8, 16
RUN = NL * TOK
WIDE = 2 * HEAD_DIM
PARTS = 4
SLICE = TOK // PARTS
CHUNK = RUN // PARTS
ROWS = GROUP * TOK
PACK = NL * SLOTS
SIDE = 16
PART = 512
FEW = 4 * SLOTS
SCALE = HEAD_DIM**-0.5
SCALE2 = SCALE / math.log(2.0)
MASKED = -1e30
F32, BF16 = jnp.float32, jnp.bfloat16


def dot_nt(a, b):
    return lax.dot_general(a, b, (((1,), (1,)), ((), ())), preferred_element_type=F32)


def dot_nn(a, b):
    return lax.dot_general(a, b, (((1,), (0,)), ((), ())), preferred_element_type=F32)


def dot_tn(a, b):
    return lax.dot_general(a, b, (((0,), (0,)), ((), ())), preferred_element_type=F32)


def remote(src, dst, sems, where):
    return pltpu.make_async_remote_copy(
        src_ref=src,
        dst_ref=dst,
        send_sem=sems[0],
        recv_sem=sems[1],
        device_id=where,
        device_id_type=MESH,
    )


def token_targets(ids, weights):
    expert = lax.broadcasted_iota(jnp.int32, (EXPERTS, TOK), 0).astype(F32)
    hits = jnp.zeros((EXPERTS, TOK), F32)
    for k in range(8):
        hits += jnp.where(ids[k : k + 1, :] == expert, 1.0, 0.0)
    rows = lax.broadcasted_iota(jnp.int32, (TOK, TOK), 0)
    cols = lax.broadcasted_iota(jnp.int32, (TOK, TOK), 1)
    before = jnp.where(rows < cols, 1.0, 0.0).astype(BF16)
    ranks = dot_nn(hits.astype(BF16), before)
    slots = [
        jnp.sum(jnp.where(ids[k : k + 1, :] == expert, ranks, 0.0), axis=0, keepdims=True)
        for k in range(8)
    ]
    slots = jnp.concatenate(slots, axis=0)
    top = jnp.concatenate([ids, slots, weights, jnp.zeros_like(ids)], axis=1)
    return jnp.concatenate([top, jnp.zeros_like(top)], axis=0).astype(BF16)


def kernel(
    q_ref, do_ref, k_ref, v_ref, mg_ref, ids_ref, comb_ref, w_ref,
    dq_ref, dk_ref, dv_ref, hid_ref,
    kv, rows, picks, snd, rcv, sums, qs, dos, stat, dqt, dkv, xs1, xr1, xs2, xr2, zs, zr,
    ring_s, ring_r, kz_s, kz_r, xf_s, xf_r, xh_s, xh_r, xb_s, xb_r, xt_s, xt_r,
    a2a_s, a2a_r, all_s, all_r, core_s, core_r, r1_s, r1_r, r2_s, r2_r, rz_s, rz_r,
):
    y = lax.axis_index("dp")
    c = lax.axis_index("ctx")
    tp = lax.axis_index("tp")
    x, zl = c // NL, c % NL
    zh, core = tp // 2, tp % 2
    z = zh * NL + zl
    plane = y * NX + x

    def at(ax, ay, az, acore):
        return (ay, ax * NL + az % NL, (az // NL) * 2 + acore)

    z_up = at(x, y, (z + 1) % NZ, core)
    z_down = at(x, y, (z + NZ - 1) % NZ, core)
    x_up = at((x + 1) % NX, y, z, core)
    x_down = at((x + NX - 1) % NX, y, z, core)
    twin = at(x, y, z, 1 - core)

    def plane_dev(d):
        return at(d % NX, d // NX, z, core)

    def line_dev(j):
        return at(x, y, zh * NL + j, core)

    barrier = pltpu.get_barrier_semaphore()

    def greet(where):
        pl.semaphore_signal(barrier, inc=1, device_id=where, device_id_type=MESH)

    greet(z_up)
    greet(z_down)
    greet(twin)

    @pl.loop(1, 16)
    def _(i):
        greet(plane_dev((plane + i) % 16))

    @pl.loop(1, NL)
    def _(i):
        greet(line_dev((zl + i) % NL))

    kv[c, :, :HEAD_DIM] = k_ref[...]
    kv[c, :, HEAD_DIM:] = v_ref[...]
    rows[8, pl.ds(SIDE, TOK), :] = mg_ref[...]
    rows[8, pl.ds(0, SIDE), :] = token_targets(
        ids_ref[...].astype(F32), comb_ref[...].astype(F32)
    )
    for h in range(GROUP):
        qs[pl.ds(h * TOK, TOK), :] = q_ref[:, h * HEAD_DIM : (h + 1) * HEAD_DIM]
        dos[pl.ds(h * TOK, TOK), :] = do_ref[:, h * HEAD_DIM : (h + 1) * HEAD_DIM]
    stat[0:1, :] = jnp.full((1, ROWS), MASKED, F32)
    stat[1:3, :] = jnp.zeros((2, ROWS), F32)
    pl.semaphore_wait(barrier, 3 + 15 + 7)

    half = (pl.ds(0, TOK // 2), pl.ds(TOK // 2, TOK // 2))
    whole = pl.ds(0, SIDE + TOK // 2)
    piece = (pl.ds(SIDE, TOK // 2), pl.ds(SIDE + TOK // 2, TOK // 2))

    def ring(way, part, s, op):
        near = (8 - s, 8 + s)[way]
        far = (7 - s, (9 + s) % NZ)[way]
        last = (3, 2)[way]

        def copy(span):
            if op != "wait_recv":
                source, target = rows.at[near, span], rows.at[far, span]
            else:
                source, target = rows.at[far, span], rows.at[far, span]
            sems = (ring_s.at[way, part, s], ring_r.at[way, part, s])
            getattr(remote(source, target, sems, (z_up, z_down)[way]), op)()

        if part == 1:
            copy(piece[1])
        else:
            pl.when(s <= last)(lambda: copy(whole))
            pl.when(s > last)(lambda: copy(piece[0]))

    def kz_copy(way, step, src):
        ref = kv.at[x * NL + src]
        return remote(ref, ref, (kz_s.at[way, step], kz_r.at[way, step]), (z_up, z_down)[way])

    def xf_copy(g, j):
        ref = kv.at[g * NL + j]
        return remote(ref, ref, (xf_s.at[j], xf_r.at[j]), x_up)

    def xh_copy(g, j):
        ref = kv.at[g * NL + j, half[0]]
        return remote(ref, ref, (xh_s.at[j], xh_r.at[j]), x_up)

    def xb_copy(part, g, j):
        ref = kv.at[g * NL + j, half[part]]
        return remote(ref, ref, (xb_s.at[part, j], xb_r.at[part, j]), x_down)

    def xt_copy(g, j):
        ref = kv.at[g * NL + j, half[1]]
        return remote(ref, ref, (xt_s.at[j], xt_r.at[j]), x_down)

    def x_send(j):
        @pl.when(x <= 2)
        def _():
            xf_copy(x, j).start()

        @pl.when(x == 0)
        def _():
            xb_copy(0, x, j).start()

        @pl.when(x <= 1)
        def _():
            xb_copy(1, x, j).start()

    lane = lax.broadcasted_iota(jnp.int32, (1, ROWS), 1) % TOK

    def scores(slot, count, first):
        size = count * TOK
        block = kv[pl.ds(slot, count)].reshape(size, WIDE)
        keys, values = block[:, :HEAD_DIM], block[:, HEAD_DIM:]
        s = dot_nt(keys, qs[...]) * SCALE2
        if first is not None:
            place = lax.broadcasted_iota(jnp.int32, (size, ROWS), 0)
            s = jnp.where(place <= lane + first, s, MASKED)
        return keys, s, dot_nt(values, dos[...])

    def stats(slot, count, first=None):
        _, s, dp = scores(slot, count, first)
        top = stat[0:1, :]
        new_top = jnp.maximum(top, jnp.max(s, axis=0, keepdims=True))
        e = jnp.exp2(s - new_top)
        shrink = jnp.exp2(top - new_top)
        stat[0:1, :] = new_top
        stat[1:2, :] = stat[1:2, :] * shrink + jnp.sum(e, axis=0, keepdims=True)
        stat[2:3, :] = stat[2:3, :] * shrink + jnp.sum(e * dp, axis=0, keepdims=True)

    def x_pass(j):
        @pl.when((j >= 0) & (j < NL))
        def _():
            @pl.when(x >= 1)
            def _():
                xf_copy(x - 1, j).wait_recv()

            @pl.when((x == 1) | (x == 2))
            def _():
                xh_copy(x - 1, j).start()

            @pl.when(x == 3)
            def _():
                xb_copy(0, 0, j).wait_recv()

            @pl.when((x == 3) | (x == 0))
            def _():
                xb_copy(1, (x + 1) % NX, j).wait_recv()
                xt_copy((x + 1) % NX, j).start()

            @pl.when(x >= 1)
            def _():
                stats((x - 1) * NL + j, 1)

            @pl.when(x == 3)
            def _():
                stats(j, 1)

    pick_row = lax.broadcasted_iota(jnp.int32, (16, TOK), 0)
    pick_sub = lax.broadcasted_iota(jnp.int32, (8, TOK), 0)

    def window(w):
        first = jnp.where(w == 0, 6, jnp.where(w == 1, 4, jnp.where(w == 2, 12, 14)))
        return first, (first + jnp.where(w == 0, 2, jnp.where(w == 3, 2, 6))) % NZ

    def make_pick(w, r):
        d = (plane + r + 1) % 16
        expert = (d // NX) * (NX * NL) + (d % NX) * NL + zl
        key = jnp.where(pick_row < SLOTS, expert * SLOTS + pick_row, -1).astype(F32)
        start = window(w)
        columns = []
        for j in range(4):
            named = rows[start[j // 2] + j % 2, pl.ds(0, SIDE), :].astype(F32)
            target = named[:8, :TOK] * float(SLOTS) + named[:8, TOK : 2 * TOK]
            weight = named[:8, 2 * TOK : 3 * TOK]
            chosen = jnp.zeros((16, TOK), F32)
            for k in range(8):
                chosen += jnp.where(target[k : k + 1, :] == key, weight[k : k + 1, :], 0.0)
            column = [
                jnp.where(pick_sub == j, chosen[i : i + 1, :], 0.0)
                + jnp.where(pick_sub == 4 + j, chosen[i + 1 : i + 2, :], 0.0)
                for i in range(0, SLOTS, 2)
            ]
            columns.append(jnp.concatenate(column, axis=0))
        picks[w, r] = jnp.concatenate(columns, axis=1)

    def a2a_out(w, r):
        return remote(
            snd.at[w, r], rcv.at[core, w, plane], (a2a_s.at[w, r], a2a_r.at[w, plane]),
            plane_dev((plane + r + 1) % 16),
        )

    def a2a_in(w, d):
        return remote(
            snd.at[w, 0], rcv.at[core, w, d], (a2a_s.at[w, 0], a2a_r.at[w, d]), plane_dev(d)
        )

    def pack_rows(w, n):
        @pl.when(w < 2)
        def _():
            @pl.loop(0, 8)
            def _(i):
                make_pick(w, n * 8 + i)

        group = jnp.where(w < 2, w, 3 - w)
        total = jnp.zeros((8 * FEW, PART), F32)
        for m, start in enumerate(window(w)):
            source = rows[pl.ds(start, 2), SIDE:, :].reshape(2 * TOK, PART)
            chosen = picks[group, pl.ds(n * 8, 8), :, m * 2 * TOK : (m + 1) * 2 * TOK]
            total += dot_nn(chosen.reshape(8 * FEW, 2 * TOK).astype(BF16), source)
        for i in range(8):
            mine = total[i * FEW : (i + 1) * FEW]
            mine = jnp.concatenate([mine[:, : PART // 2], mine[:, PART // 2 :]], axis=0)
            snd[w, n * 8 + i] = mine.astype(BF16)

        @pl.when(n == 1)
        def _():
            rcv[core, w, plane] = snd[w, 15]

    def launch_rows(w, n):
        @pl.loop(0, 8)
        def _(i):
            @pl.when(n * 8 + i < 15)
            def _():
                a2a_out(w, n * 8 + i).start()

    @pl.when(zl < NL - 1)
    def _():
        kz_copy(0, 0, zl).start()

    @pl.when(zl > 0)
    def _():
        kz_copy(1, 0, zl).start()

    x_send(zl)
    ring(0, 0, 0, "start")
    ring(1, 1, 0, "start")
    ring(0, 1, 0, "start")
    ring(1, 0, 0, "start")
    stats(c, 1, 0)

    @pl.loop(0, NL + 1)
    def _(s):
        below, above = zl - 1 - s, zl + 1 + s

        @pl.when(below >= 0)
        def _():
            kz_copy(0, s, below).wait_recv()

            @pl.when(zl < NL - 1)
            def _():
                kz_copy(0, s + 1, below).start()

        @pl.when(above < NL)
        def _():
            kz_copy(1, s, above).wait_recv()

            @pl.when(zl > 0)
            def _():
                kz_copy(1, s + 1, above).start()

        @pl.when(below >= 0)
        def _():
            x_send(below)

        @pl.when(above < NL)
        def _():
            x_send(above)

        @pl.when(below >= 0)
        def _():
            stats(x * NL + below, 1)

        for way, part in ((0, 0), (1, 1), (0, 1), (1, 0)):
            most = NL if way == part else NL - 1

            @pl.when((s >= 1) & (s <= most))
            def _():
                ring(way, part, s - 1, "wait_recv")

                @pl.when(s < most)
                def _():
                    ring(way, part, s, "start")

        @pl.when(s == 1)
        def _():
            x_pass(zl)

        @pl.when(s >= 1)
        def _():
            x_pass(zl - s)
            x_pass(zl + s)

        @pl.when((s >= 2) & (s < NL))
        def _():
            pack_rows((s - 2) // 2, s % 2)

        @pl.when((s >= 2) & (s < 6))
        def _():
            launch_rows((s - 2) // 2, s % 2)

    @pl.loop(0, 2)
    def _(n):
        launch_rows(2, n)

    @pl.when(x == 0)
    def _():
        @pl.loop(0, 2)
        def _(n):
            pack_rows(3, n)
            launch_rows(3, n)

    @pl.when(x >= 2)
    def _():
        @pl.loop(0, NL)
        def _(j):
            xh_copy(x - 2, j).wait_recv()
            xt_copy(x - 2, j).wait_recv()

        @pl.loop(0, 2)
        def _(i):
            stats((x - 2) * NL + i * 4, 4)

    stat[2:3, :] = stat[2:3, :] / stat[1:2, :]
    stat[0:1, :] = stat[0:1, :] + jnp.log2(stat[1:2, :])
    dqt[...] = jnp.zeros_like(dqt)
    def grads(g, part, masked=False):
        here = pl.ds(pl.multiple_of(part * SLICE, SLICE), SLICE)
        block = kv[pl.ds(g * NL, NL), here, :].reshape(CHUNK, WIDE)
        keys, values = block[:, :HEAD_DIM], block[:, HEAD_DIM:]
        s = dot_nt(keys, qs[...]) * SCALE2
        if masked:
            row = lax.broadcasted_iota(jnp.int32, (CHUNK, ROWS), 0)
            place = row // SLICE * TOK + row % SLICE
            s = jnp.where(place <= lane + (zl * TOK - part * SLICE), s, MASKED)
        dp = dot_nt(values, dos[...])
        p = jnp.exp2(s - stat[0:1, :])
        ds = (p * (dp - stat[2:3, :])).astype(BF16)
        dkv[g, part, :, HEAD_DIM:] = dot_nn(p.astype(BF16), dos[...])
        dkv[g, part, :, :HEAD_DIM] = dot_nn(ds, qs[...])
        dqt[...] += dot_tn(keys, ds)

    def r1_copy(way, part):
        return remote(
            xs1.at[part], xr1.at[part], (r1_s.at[part], r1_r.at[part]), (x_up, x_down)[way]
        )

    def r2_copy(way, part, src=None):
        ref = xs2.at[way, part] if src is None else src
        return remote(
            ref, xr2.at[way, part], (r2_s.at[way, part], r2_r.at[way, part]), (x_up, x_down)[way]
        )

    def rz_send(part, j):
        return remote(
            zs.at[part, j], zr.at[part, zl], (rz_s.at[part, j], rz_r.at[part, zl]), line_dev(j)
        )

    def rz_got(part, j):
        return remote(
            zs.at[part, j], zr.at[part, j], (rz_s.at[part, j], rz_r.at[part, j]), line_dev(j)
        )

    def z_spread(part):
        zs[part] = dkv[x, part].astype(BF16).reshape(NL, SLICE, WIDE)

        @pl.loop(1, NL)
        def _(i):
            rz_send(part, (zl + i) % NL).start()

    @pl.when(x >= 2)
    def _():
        @pl.loop(0, 4)
        def _(part):
            grads(x - 2, part)
            xs1[part] = dkv[x - 2, part].astype(BF16)
            pl.when(part < 2)(lambda: r1_copy(0, part).start())
            pl.when(part >= 2)(lambda: r1_copy(1, part).start())

    @pl.when(x == 3)
    def _():
        @pl.loop(0, 4)
        def _(n):
            part = (n + 2) % 4
            grads(0, part)

            @pl.when(part < 2)
            def _():
                r1_copy(0, part).wait_recv()
                dkv[0, part] += xr1[part].astype(F32)

            xs2[0, part] = dkv[0, part].astype(BF16)
            r2_copy(0, part).start()

    @pl.when(x >= 1)
    def _():
        @pl.loop(0, 4)
        def _(part):
            grads(x - 1, part)

            @pl.when((part >= 2) & (x < 3))
            def _():
                r1_copy(1, part).wait_recv()
                dkv[x - 1, part] += xr1[part].astype(F32)

            xs2[1, part] = dkv[x - 1, part].astype(BF16)
            r2_copy(1, part).start()

    @pl.loop(0, 4)
    def _(part):
        grads(x, part, True)
        pl.when(x == 3)(lambda: z_spread(part))

    @pl.when(x >= 1)
    def _():
        @pl.loop(0, 2)
        def _(n):
            pack_rows(3, n)
            launch_rows(3, n)

    @pl.when(x == 0)
    def _():
        @pl.loop(0, 2)
        def _(part):
            r1_copy(0, part).wait_recv()
            r2_copy(0, part, xr1.at[part]).start()

    for h in range(GROUP):
        at_head = slice(h * TOK, (h + 1) * TOK)
        dq_ref[:, at_head] = (dqt[:, at_head].T * SCALE).astype(BF16)

    def all_copy(side, w):
        ref = rcv.at[side, w]
        return remote(ref, ref, (all_s.at[w], all_r.at[w]), twin)

    row = lax.broadcasted_iota(jnp.int32, (8 * PACK, PART // 2), 0) % 4
    spot = row + jnp.where(row < 2, 4, 8)
    low = ((z + 14 + row) % NZ < NL, (z + 8 + spot) % NZ < NL)

    def expert_group(group):
        @pl.loop(0, 2)
        def _(i):
            total = jnp.zeros((8 * FEW, w_ref.shape[0]), F32)
            for side in range(2):
                near = rcv[side, group, pl.ds(i * 8, 8)].reshape(8 * PACK, PART // 2)
                far = rcv[side, 3 - group, pl.ds(i * 8, 8)].reshape(8 * PACK, PART // 2)
                for part in range(2):
                    a, b = (near, far) if part == 0 else (far, near)
                    left = jnp.where(low[group], a, b).astype(F32)
                    for m in range(2):
                        begin = (part * 2 + side) * PART + m * (PART // 2)
                        cuts = [
                            left[n * PACK + m * FEW : n * PACK + (m + 1) * FEW] for n in range(8)
                        ]
                        total += dot_nt(
                            jnp.concatenate(cuts, axis=0).astype(BF16),
                            w_ref[:, begin : begin + PART // 2],
                        )
            sums[group, pl.ds(pl.multiple_of(i * 8 * FEW, 8), 8 * FEW), :] = total

    def core_copy(side, d):
        ref = rcv.at[side, 3, d]
        return remote(ref, ref, (core_s.at[d], core_r.at[d]), twin)

    def swap_rows(w):
        @pl.loop(1, 16)
        def _(i):
            a2a_in(w, (plane + 16 - i) % 16).wait_recv()

        all_copy(core, w).start()

    pl.loop(0, 3)(swap_rows)

    @pl.loop(0, 4)
    def _(part):
        @pl.when(x <= 2)
        def _():
            r2_copy(1, part).wait_recv()
            dkv[x, part] += xr2[1, part].astype(F32)

            @pl.when((x == 0) | ((x == 1) & (part < 2)))
            def _():
                r2_copy(0, part).wait_recv()
                dkv[x, part] += xr2[0, part].astype(F32)

            z_spread(part)

    @pl.loop(1, 3)
    def _(w):
        all_copy(1 - core, w).wait_recv()

    expert_group(1)
    core_copy(core, plane).start()

    @pl.loop(1, 16)
    def _(i):
        d = (plane + 16 - i) % 16
        a2a_in(3, d).wait_recv()
        core_copy(core, d).start()

    @pl.loop(0, 16)
    def _(i):
        core_copy(1 - core, (plane + 16 - i) % 16).wait_recv()

    all_copy(1 - core, 0).wait_recv()
    expert_group(0)

    goal = lax.broadcasted_iota(jnp.int32, (PACK, PACK), 0)
    have = lax.broadcasted_iota(jnp.int32, (PACK, PACK), 1)
    have_row = have % 4
    have_spot = jnp.where(have < FEW, have_row + 6, have_row + jnp.where(have_row < 2, 4, 8))
    fits = (goal // NL == have % FEW // 4) & (goal % NL == (zl + have_spot) % NL)
    order = jnp.where(fits, 1.0, 0.0).astype(BF16)

    @pl.loop(0, 4)
    def _(i):
        outs = []
        for n in range(4):
            at_rows = pl.ds(pl.multiple_of((i * 4 + n) * FEW, 8), FEW)
            both = [sums[0, at_rows, :], sums[1, at_rows, :]]
            outs.append(dot_nn(order, jnp.concatenate(both, axis=0).astype(BF16)))
        for n in range(SLOTS):
            parts = [out[n * NL : (n + 1) * NL, :] for out in outs]
            here = pl.ds(pl.multiple_of(i * 4 * NL, 4 * NL), 4 * NL)
            hid_ref[n, here, :] = jnp.concatenate(parts, axis=0).astype(BF16)

    @pl.loop(0, PARTS)
    def _(part):
        own = dkv[x, part, pl.ds(pl.multiple_of(zl * SLICE, SLICE), SLICE), :]
        for i in range(1, NL):
            j = (zl + i) % NL
            rz_got(part, j).wait_recv()
            own += zr[part, j].astype(F32)
        here = pl.ds(pl.multiple_of(part * SLICE, SLICE), SLICE)
        dk_ref[here, :] = (own[:, :HEAD_DIM] * SCALE).astype(BF16)
        dv_ref[here, :] = own[:, HEAD_DIM:].astype(BF16)

    @pl.loop(0, NL)
    def _(s):
        @pl.when((zl < NL - 1) & (zl - s >= 0))
        def _():
            kz_copy(0, s, zl - s).wait_send()

        @pl.when((zl > 0) & (zl + s < NL))
        def _():
            kz_copy(1, s, zl + s).wait_send()

        ring(0, 0, s, "wait_send")
        ring(1, 1, s, "wait_send")

        @pl.when(s < NL - 1)
        def _():
            ring(0, 1, s, "wait_send")
            ring(1, 0, s, "wait_send")

        @pl.when(x <= 2)
        def _():
            xf_copy(x, s).wait_send()

        @pl.when(x == 0)
        def _():
            xb_copy(0, x, s).wait_send()

        @pl.when(x <= 1)
        def _():
            xb_copy(1, x, s).wait_send()

        @pl.when((x == 1) | (x == 2))
        def _():
            xh_copy(x - 1, s).wait_send()

        @pl.when((x == 3) | (x == 0))
        def _():
            xt_copy((x + 1) % NX, s).wait_send()

    @pl.loop(0, 3)
    def _(w):
        all_copy(core, w).wait_send()

    core_copy(core, plane).wait_send()

    @pl.loop(0, 15)
    def _(r):
        for w in range(4):
            a2a_out(w, r).wait_send()
        core_copy(core, (plane + r + 1) % 16).wait_send()

    @pl.loop(0, 4)
    def _(part):
        @pl.when(x >= 2)
        def _():
            pl.when(part < 2)(lambda: r1_copy(0, part).wait_send())
            pl.when(part >= 2)(lambda: r1_copy(1, part).wait_send())

        @pl.when(x >= 1)
        def _():
            r2_copy(1, part).wait_send()

        @pl.when((x == 3) | ((x == 0) & (part < 2)))
        def _():
            r2_copy(0, part).wait_send()

    @pl.loop(1, NL)
    def _(i):
        for part in range(PARTS):
            rz_send(part, (zl + i) % NL).wait_send()


def place(*refs):
    for source, target in zip(refs[:4], refs[4:]):
        target[...] = source[...]


def per_device(queries, keys, values, out_grad, mixed_grad, expert_ids, combine, w_down):
    vmem = pl.BlockSpec(memory_space=pltpu.VMEM)
    dma = pltpu.SemaphoreType.DMA
    hid = w_down.shape[1]
    shapes = (
        jax.ShapeDtypeStruct((TOK, ROWS), BF16),
        jax.ShapeDtypeStruct((TOK, HEAD_DIM), BF16),
        jax.ShapeDtypeStruct((TOK, HEAD_DIM), BF16),
        jax.ShapeDtypeStruct((SLOTS, EXPERTS, hid), BF16),
    )
    scratch = [
        pltpu.VMEM((NX * NL, TOK, WIDE), BF16),
        pltpu.VMEM((NZ, SIDE + TOK, PART), BF16),
        pltpu.VMEM((2, 16, FEW, PART), F32),
        pltpu.VMEM((4, 16, PACK, PART // 2), BF16),
        pltpu.VMEM((2, 4, 16, PACK, PART // 2), BF16),
        pltpu.VMEM((2, 16 * FEW, hid), F32),
        pltpu.VMEM((ROWS, HEAD_DIM), BF16),
        pltpu.VMEM((ROWS, HEAD_DIM), BF16),
        pltpu.VMEM((8, ROWS), F32),
        pltpu.VMEM((HEAD_DIM, ROWS), F32),
        pltpu.VMEM((NX, PARTS, CHUNK, WIDE), F32),
        pltpu.VMEM((4, CHUNK, WIDE), BF16),
        pltpu.VMEM((4, CHUNK, WIDE), BF16),
        pltpu.VMEM((2, 4, CHUNK, WIDE), BF16),
        pltpu.VMEM((2, 4, CHUNK, WIDE), BF16),
        pltpu.VMEM((PARTS, NL, SLICE, WIDE), BF16),
        pltpu.VMEM((PARTS, NL, SLICE, WIDE), BF16),
    ]
    for shape in (
        (2, 2, NL), (2, NL), (NL,), (NL,), (2, NL), (NL,),
        (4, 16), (3,), (16,), (4,), (2, 4), (PARTS, NL),
    ):
        scratch += [dma(shape), dma(shape)]
    dq, dk, dv, hidden = pl.pallas_call(
        kernel,
        out_shape=shapes,
        in_specs=[vmem] * 8,
        out_specs=(vmem,) * 4,
        scratch_shapes=scratch,
        compiler_params=pltpu.CompilerParams(
            collective_id=0, has_side_effects=True, vmem_limit_bytes=56 * 1024 * 1024
        ),
        name="layer_backward",
    )(queries[0], out_grad[0], keys[0], values[0], mixed_grad, expert_ids.T, combine.T, w_down[0])
    dq, dk, dv, hidden = pl.pallas_call(
        place,
        out_shape=shapes,
        in_specs=[vmem] * 4,
        out_specs=(vmem,) * 4,
        name="place_outputs",
    )(dq, dk, dv, hidden)
    return dq[None], dk[None], dv[None], hidden.transpose(1, 0, 2)[None]


def solution(mesh):
    placed = (
        P("dp", "ctx", "tp"),
        P("dp", "ctx", "tp"),
        P("dp", "ctx", "tp"),
        P("dp", "ctx", "tp"),
        P(("dp", "ctx"), "tp"),
        P(("dp", "ctx"), None),
        P(("dp", "ctx"), None),
        P(("dp", "ctx"), "tp", None),
    )
    return jax.shard_map(
        per_device,
        mesh=mesh,
        in_specs=placed,
        out_specs=(
            P("dp", "ctx", "tp"),
            P("dp", "ctx", "tp"),
            P("dp", "ctx", "tp"),
            P(("dp", "ctx"), None, None, "tp"),
        ),
        check_vma=False,
    )
```

```python
import functools
import math

import jax
import jax.numpy as jnp
from jax import lax
from jax.experimental import pallas as pl
from jax.experimental.pallas import tpu as pltpu
from jax.sharding import PartitionSpec as P

MESH = pl.DeviceIdType.MESH
HEAD_DIM = 128
GROUP = 8
TOK = 128
SLOTS = 10
EXPERTS = 128
NX, NY, NL, NZ = 4, 4, 8, 16
RUN = NL * TOK
WIDE = 2 * HEAD_DIM
PARTS = 4
SLICE = TOK // PARTS
CHUNK = RUN // PARTS
ROWS = GROUP * TOK
PACK = NL * SLOTS
SIDE = 16
PART = 512
FEW = 4 * SLOTS
SCALE = HEAD_DIM**-0.5
SCALE2 = SCALE / math.log(2.0)
MASKED = -1e30
F32, BF16 = jnp.float32, jnp.bfloat16


def dot_nt(a, b):
    return lax.dot_general(a, b, (((1,), (1,)), ((), ())), preferred_element_type=F32)


def dot_nn(a, b):
    return lax.dot_general(a, b, (((1,), (0,)), ((), ())), preferred_element_type=F32)


def dot_tn(a, b):
    return lax.dot_general(a, b, (((0,), (0,)), ((), ())), preferred_element_type=F32)


def remote(src, dst, sems, where):
    return pltpu.make_async_remote_copy(
        src_ref=src,
        dst_ref=dst,
        send_sem=sems[0],
        recv_sem=sems[1],
        device_id=where,
        device_id_type=MESH,
    )


def token_targets(ids, weights):
    expert = lax.broadcasted_iota(jnp.int32, (EXPERTS, TOK), 0).astype(F32)
    hits = jnp.zeros((EXPERTS, TOK), F32)
    for k in range(8):
        hits += jnp.where(ids[k : k + 1, :] == expert, 1.0, 0.0)
    rows = lax.broadcasted_iota(jnp.int32, (TOK, TOK), 0)
    cols = lax.broadcasted_iota(jnp.int32, (TOK, TOK), 1)
    before = jnp.where(rows < cols, 1.0, 0.0).astype(BF16)
    ranks = dot_nn(hits.astype(BF16), before)
    slots = [
        jnp.sum(jnp.where(ids[k : k + 1, :] == expert, ranks, 0.0), axis=0, keepdims=True)
        for k in range(8)
    ]
    slots = jnp.concatenate(slots, axis=0)
    top = jnp.concatenate([ids, slots, weights, jnp.zeros_like(ids)], axis=1)
    return jnp.concatenate([top, jnp.zeros_like(top)], axis=0).astype(BF16)


def kernel(
    q_ref, do_ref, k_ref, v_ref, mg_ref, ids_ref, comb_ref, w_ref,
    dq_ref, dk_ref, dv_ref, hid_ref,
    kv, rows, picks, snd, rcv, sums, qs, dos, stat, dqt, dkv, xs1, xr1, xs2, xr2, zs, za, zb, zr,
    ring_s, ring_r, kz_s, kz_r, xf_s, xf_r, xh_s, xh_r, xb_s, xb_r, xt_s, xt_r,
    a2a_s, a2a_r, all_s, all_r, core_s, core_r, r1_s, r1_r, r2_s, r2_r, za_s, za_r, rz_s, rz_r,
):
    y = lax.axis_index("dp")
    c = lax.axis_index("ctx")
    tp = lax.axis_index("tp")
    x, zl = c // NL, c % NL
    zh, core = tp // 2, tp % 2
    z = zh * NL + zl
    plane = y * NX + x

    def at(ax, ay, az, acore):
        return (ay, ax * NL + az % NL, (az // NL) * 2 + acore)

    z_up = at(x, y, (z + 1) % NZ, core)
    z_down = at(x, y, (z + NZ - 1) % NZ, core)
    x_up = at((x + 1) % NX, y, z, core)
    x_down = at((x + NX - 1) % NX, y, z, core)
    twin = at(x, y, z, 1 - core)

    def plane_dev(d):
        return at(d % NX, d // NX, z, core)

    def line_dev(j):
        return at(x, y, zh * NL + j, core)

    barrier = pltpu.get_barrier_semaphore()

    def greet(where):
        pl.semaphore_signal(barrier, inc=1, device_id=where, device_id_type=MESH)

    greet(z_up)
    greet(z_down)
    greet(twin)

    @pl.loop(1, 16)
    def _(i):
        greet(plane_dev((plane + i) % 16))

    @pl.loop(1, NL)
    def _(i):
        greet(line_dev((zl + i) % NL))

    kv[c, :, :HEAD_DIM] = k_ref[...]
    kv[c, :, HEAD_DIM:] = v_ref[...]
    pl.semaphore_wait(barrier, 3 + 15 + 7)

    half = (pl.ds(0, TOK // 2), pl.ds(TOK // 2, TOK // 2))
    whole = pl.ds(0, SIDE + TOK // 2)
    piece = (pl.ds(SIDE, TOK // 2), pl.ds(SIDE + TOK // 2, TOK // 2))

    def ring(way, part, s, op):
        near = (8 - s, 8 + s)[way]
        far = (7 - s, (9 + s) % NZ)[way]
        last = (3, 2)[way]

        def copy(span):
            if op != "wait_recv":
                source, target = rows.at[near, span], rows.at[far, span]
            else:
                source, target = rows.at[far, span], rows.at[far, span]
            sems = (ring_s.at[way, part, s], ring_r.at[way, part, s])
            getattr(remote(source, target, sems, (z_up, z_down)[way]), op)()

        if part == 1:
            copy(piece[1])
        else:
            pl.when(s <= last)(lambda: copy(whole))
            pl.when(s > last)(lambda: copy(piece[0]))

    def kz_copy(way, step, src):
        ref = kv.at[x * NL + src]
        return remote(ref, ref, (kz_s.at[way, step], kz_r.at[way, step]), (z_up, z_down)[way])

    def xf_copy(g, j):
        ref = kv.at[g * NL + j]
        return remote(ref, ref, (xf_s.at[j], xf_r.at[j]), x_up)

    def xh_copy(g, j):
        ref = kv.at[g * NL + j, half[0]]
        return remote(ref, ref, (xh_s.at[j], xh_r.at[j]), x_up)

    def xb_copy(part, g, j):
        ref = kv.at[g * NL + j, half[part]]
        return remote(ref, ref, (xb_s.at[part, j], xb_r.at[part, j]), x_down)

    def xt_copy(g, j):
        ref = kv.at[g * NL + j, half[1]]
        return remote(ref, ref, (xt_s.at[j], xt_r.at[j]), x_down)

    def x_send(j):
        @pl.when(x <= 2)
        def _():
            xf_copy(x, j).start()

        @pl.when(x == 0)
        def _():
            xb_copy(0, x, j).start()

        @pl.when(x <= 1)
        def _():
            xb_copy(1, x, j).start()

    lane = lax.broadcasted_iota(jnp.int32, (1, ROWS), 1) % TOK

    def scores(slot, count, first):
        size = count * TOK
        block = kv[pl.ds(slot, count)].reshape(size, WIDE)
        keys, values = block[:, :HEAD_DIM], block[:, HEAD_DIM:]
        s = dot_nt(keys, qs[...]) * SCALE2
        if first is not None:
            place = lax.broadcasted_iota(jnp.int32, (size, ROWS), 0)
            s = jnp.where(place <= lane + first, s, MASKED)
        return keys, s, dot_nt(values, dos[...])

    def stats(slot, count, first=None):
        _, s, dp = scores(slot, count, first)
        top = stat[0:1, :]
        new_top = jnp.maximum(top, jnp.max(s, axis=0, keepdims=True))
        e = jnp.exp2(s - new_top)
        shrink = jnp.exp2(top - new_top)
        stat[0:1, :] = new_top
        stat[1:2, :] = stat[1:2, :] * shrink + jnp.sum(e, axis=0, keepdims=True)
        stat[2:3, :] = stat[2:3, :] * shrink + jnp.sum(e * dp, axis=0, keepdims=True)

    def x_pass(j):
        @pl.when((j >= 0) & (j < NL))
        def _():
            @pl.when(x >= 1)
            def _():
                xf_copy(x - 1, j).wait_recv()

            @pl.when((x == 1) | (x == 2))
            def _():
                xh_copy(x - 1, j).start()

            @pl.when(x == 3)
            def _():
                xb_copy(0, 0, j).wait_recv()

            @pl.when((x == 3) | (x == 0))
            def _():
                xb_copy(1, (x + 1) % NX, j).wait_recv()
                xt_copy((x + 1) % NX, j).start()

            @pl.when(x >= 1)
            def _():
                stats((x - 1) * NL + j, 1)

            @pl.when(x == 3)
            def _():
                stats(j, 1)

    pick_row = lax.broadcasted_iota(jnp.int32, (16, TOK), 0)
    pick_sub = lax.broadcasted_iota(jnp.int32, (8, TOK), 0)

    def window(w):
        first = jnp.where(w == 0, 6, jnp.where(w == 1, 4, jnp.where(w == 2, 12, 14)))
        return first, (first + jnp.where(w == 0, 2, jnp.where(w == 3, 2, 6))) % NZ

    def make_pick(w, r):
        d = (plane + r + 1) % 16
        expert = (d // NX) * (NX * NL) + (d % NX) * NL + zl
        key = jnp.where(pick_row < SLOTS, expert * SLOTS + pick_row, -1).astype(F32)
        start = window(w)
        columns = []
        for j in range(4):
            named = rows[start[j // 2] + j % 2, pl.ds(0, SIDE), :].astype(F32)
            target = named[:8, :TOK] * float(SLOTS) + named[:8, TOK : 2 * TOK]
            weight = named[:8, 2 * TOK : 3 * TOK]
            chosen = jnp.zeros((16, TOK), F32)
            for k in range(8):
                chosen += jnp.where(target[k : k + 1, :] == key, weight[k : k + 1, :], 0.0)
            column = [
                jnp.where(pick_sub == j, chosen[i : i + 1, :], 0.0)
                + jnp.where(pick_sub == 4 + j, chosen[i + 1 : i + 2, :], 0.0)
                for i in range(0, SLOTS, 2)
            ]
            columns.append(jnp.concatenate(column, axis=0))
        picks[w, r] = jnp.concatenate(columns, axis=1)

    def a2a_out(w, r):
        return remote(
            snd.at[w, r], rcv.at[core, w, plane], (a2a_s.at[w, r], a2a_r.at[w, plane]),
            plane_dev((plane + r + 1) % 16),
        )

    def a2a_in(w, d):
        return remote(
            snd.at[w, 0], rcv.at[core, w, d], (a2a_s.at[w, 0], a2a_r.at[w, d]), plane_dev(d)
        )

    def pack_rows(w, n):
        @pl.when(w < 2)
        def _():
            @pl.loop(0, 8)
            def _(i):
                make_pick(w, n * 8 + i)

        group = jnp.where(w < 2, w, 3 - w)
        total = jnp.zeros((8 * FEW, PART), F32)
        for m, start in enumerate(window(w)):
            source = rows[pl.ds(start, 2), SIDE:, :].reshape(2 * TOK, PART)
            chosen = picks[group, pl.ds(n * 8, 8), :, m * 2 * TOK : (m + 1) * 2 * TOK]
            total += dot_nn(chosen.reshape(8 * FEW, 2 * TOK).astype(BF16), source)
        for i in range(8):
            mine = total[i * FEW : (i + 1) * FEW]
            mine = jnp.concatenate([mine[:, : PART // 2], mine[:, PART // 2 :]], axis=0)
            snd[w, n * 8 + i] = mine.astype(BF16)

        @pl.when(n == 1)
        def _():
            rcv[core, w, plane] = snd[w, 15]

    def launch_rows(w, n):
        @pl.loop(0, 8)
        def _(i):
            @pl.when(n * 8 + i < 15)
            def _():
                a2a_out(w, n * 8 + i).start()

    @pl.when(zl < NL - 1)
    def _():
        kz_copy(0, 0, zl).start()

    @pl.when(zl > 0)
    def _():
        kz_copy(1, 0, zl).start()

    x_send(zl)
    rows[8, pl.ds(SIDE, TOK), :] = mg_ref[...]
    rows[8, pl.ds(0, SIDE), :] = token_targets(
        ids_ref[...].astype(F32), comb_ref[...].astype(F32)
    )
    for h in range(GROUP):
        qs[pl.ds(h * TOK, TOK), :] = q_ref[:, h * HEAD_DIM : (h + 1) * HEAD_DIM]
        dos[pl.ds(h * TOK, TOK), :] = do_ref[:, h * HEAD_DIM : (h + 1) * HEAD_DIM]
    stat[0:1, :] = jnp.full((1, ROWS), MASKED, F32)
    stat[1:3, :] = jnp.zeros((2, ROWS), F32)
    ring(0, 0, 0, "start")
    ring(1, 1, 0, "start")
    ring(0, 1, 0, "start")
    ring(1, 0, 0, "start")
    stats(c, 1, 0)

    @pl.loop(0, NL)
    def _(s):
        below, above = zl - 1 - s, zl + 1 + s

        @pl.when(below >= 0)
        def _():
            kz_copy(0, s, below).wait_recv()

            @pl.when(zl < NL - 1)
            def _():
                kz_copy(0, s + 1, below).start()

        @pl.when(above < NL)
        def _():
            kz_copy(1, s, above).wait_recv()

            @pl.when(zl > 0)
            def _():
                kz_copy(1, s + 1, above).start()

        @pl.when(below >= 0)
        def _():
            x_send(below)

        @pl.when(above < NL)
        def _():
            x_send(above)

        @pl.when(below >= 0)
        def _():
            stats(x * NL + below, 1)

        for way, part in ((0, 0), (1, 1), (0, 1), (1, 0)):
            most = NL if way == part else NL - 1

            @pl.when(s >= 1)
            def _():
                ring(way, part, s - 1, "wait_recv")

                @pl.when(s < most)
                def _():
                    ring(way, part, s, "start")

        @pl.when(s == 1)
        def _():
            x_pass(zl)

        @pl.when(s >= 1)
        def _():
            x_pass(zl - s)
            x_pass(zl + s)

        @pl.when(s >= 2)
        def _():
            pack_rows((s - 2) // 2, s % 2)

        @pl.when((s >= 2) & (s < 6))
        def _():
            launch_rows((s - 2) // 2, s % 2)

    @pl.loop(0, 2)
    def _(n):
        launch_rows(2, n)

    @pl.when(x == 0)
    def _():
        ring(0, 0, NL - 1, "wait_recv")
        ring(1, 1, NL - 1, "wait_recv")

        @pl.loop(0, 2)
        def _(n):
            pack_rows(3, n)
            launch_rows(3, n)

    @pl.when(x >= 2)
    def _():
        @pl.loop(0, NL)
        def _(j):
            xh_copy(x - 2, j).wait_recv()
            xt_copy(x - 2, j).wait_recv()

        @pl.loop(0, 2)
        def _(i):
            stats((x - 2) * NL + i * 4, 4)

    stat[2:3, :] = stat[2:3, :] / stat[1:2, :]
    stat[0:1, :] = stat[0:1, :] + jnp.log2(stat[1:2, :])
    dqt[...] = jnp.zeros_like(dqt)
    def grads(g, part, masked=False):
        here = pl.ds(pl.multiple_of(part * SLICE, SLICE), SLICE)
        block = kv[pl.ds(g * NL, NL), here, :].reshape(CHUNK, WIDE)
        keys, values = block[:, :HEAD_DIM], block[:, HEAD_DIM:]
        s = dot_nt(keys, qs[...]) * SCALE2
        if masked:
            row = lax.broadcasted_iota(jnp.int32, (CHUNK, ROWS), 0)
            place = row // SLICE * TOK + row % SLICE
            s = jnp.where(place <= lane + (zl * TOK - part * SLICE), s, MASKED)
        dp = dot_nt(values, dos[...])
        p = jnp.exp2(s - stat[0:1, :])
        ds = (p * (dp - stat[2:3, :])).astype(BF16)
        dkv[g, part, :, HEAD_DIM:] = dot_nn(p.astype(BF16), dos[...])
        dkv[g, part, :, :HEAD_DIM] = dot_nn(ds, qs[...])
        dqt[...] += dot_tn(keys, ds)

    def r1_copy(way, part):
        return remote(
            xs1.at[part], xr1.at[part], (r1_s.at[part], r1_r.at[part]), (x_up, x_down)[way]
        )

    def r2_copy(way, part, src=None):
        ref = xs2.at[way, part] if src is None else src
        return remote(
            ref, xr2.at[way, part], (r2_s.at[way, part], r2_r.at[way, part]), (x_up, x_down)[way]
        )

    side, mine = zl % 2, zl // 2

    def block_rows(j):
        return pl.ds(pl.multiple_of(j * SLICE, SLICE), SLICE)

    def pair_copy(part):
        sems = (za_s.at[part], za_r.at[part])
        return remote(zs.at[part], za.at[part], sems, line_dev(zl + 1 - 2 * side))

    def rz_send(part, n):
        return remote(
            zb.at[part, n], zr.at[part, mine], (rz_s.at[part, n], rz_r.at[part, mine]),
            line_dev(2 * n + side),
        )

    def rz_got(part, n):
        return remote(
            zb.at[part, n], zr.at[part, n], (rz_s.at[part, n], rz_r.at[part, n]),
            line_dev(2 * n + side),
        )

    def z_spread(part):
        for n in range(4):
            zs[part, n] = dkv[x, part, block_rows(2 * n + 1 - side), :].astype(BF16)
        pair_copy(part).start()

    def z_relay(part):
        pair_copy(part).wait_recv()
        for n in range(4):
            total = dkv[x, part, block_rows(2 * n + side), :] + za[part, n].astype(F32)
            dkv[x, part, block_rows(2 * n + side), :] = total
            zb[part, n] = total.astype(BF16)

        @pl.loop(1, 4)
        def _(i):
            rz_send(part, (mine + i) % 4).start()

    @pl.when(x >= 2)
    def _():
        @pl.loop(0, 4)
        def _(part):
            grads(x - 2, part)
            xs1[part] = dkv[x - 2, part].astype(BF16)
            pl.when(part < 2)(lambda: r1_copy(0, part).start())
            pl.when(part >= 2)(lambda: r1_copy(1, part).start())

    @pl.when(x == 3)
    def _():
        @pl.loop(0, 4)
        def _(n):
            part = (n + 2) % 4
            grads(0, part)

            @pl.when(part < 2)
            def _():
                r1_copy(0, part).wait_recv()
                dkv[0, part] += xr1[part].astype(F32)

            xs2[0, part] = dkv[0, part].astype(BF16)
            r2_copy(0, part).start()

    @pl.when(x >= 1)
    def _():
        @pl.loop(0, 4)
        def _(part):
            grads(x - 1, part)

            @pl.when((part >= 2) & (x < 3))
            def _():
                r1_copy(1, part).wait_recv()
                dkv[x - 1, part] += xr1[part].astype(F32)

            xs2[1, part] = dkv[x - 1, part].astype(BF16)
            r2_copy(1, part).start()

    @pl.loop(0, 4)
    def _(part):
        grads(x, part, True)
        pl.when(x == 3)(lambda: z_spread(part))

    @pl.when(x >= 1)
    def _():
        ring(0, 0, NL - 1, "wait_recv")
        ring(1, 1, NL - 1, "wait_recv")

        @pl.loop(0, 2)
        def _(n):
            pack_rows(3, n)
            launch_rows(3, n)

    @pl.when(x == 0)
    def _():
        @pl.loop(0, 2)
        def _(part):
            r1_copy(0, part).wait_recv()
            r2_copy(0, part, xr1.at[part]).start()

    for h in range(GROUP):
        at_head = slice(h * TOK, (h + 1) * TOK)
        dq_ref[:, at_head] = (dqt[:, at_head].T * SCALE).astype(BF16)

    def all_copy(side, w):
        ref = rcv.at[side, w]
        return remote(ref, ref, (all_s.at[w], all_r.at[w]), twin)

    row = lax.broadcasted_iota(jnp.int32, (8 * PACK, PART // 2), 0) % 4
    spot = row + jnp.where(row < 2, 4, 8)
    low = ((z + 14 + row) % NZ < NL, (z + 8 + spot) % NZ < NL)

    def expert_group(group):
        @pl.loop(0, 2)
        def _(i):
            total = jnp.zeros((8 * FEW, w_ref.shape[0]), F32)
            for side in range(2):
                near = rcv[side, group, pl.ds(i * 8, 8)].reshape(8 * PACK, PART // 2)
                far = rcv[side, 3 - group, pl.ds(i * 8, 8)].reshape(8 * PACK, PART // 2)
                for part in range(2):
                    a, b = (near, far) if part == 0 else (far, near)
                    left = jnp.where(low[group], a, b).astype(F32)
                    for m in range(2):
                        begin = (part * 2 + side) * PART + m * (PART // 2)
                        cuts = [
                            left[n * PACK + m * FEW : n * PACK + (m + 1) * FEW] for n in range(8)
                        ]
                        total += dot_nt(
                            jnp.concatenate(cuts, axis=0).astype(BF16),
                            w_ref[:, begin : begin + PART // 2],
                        )
            sums[group, pl.ds(pl.multiple_of(i * 8 * FEW, 8), 8 * FEW), :] = total

    def core_copy(side, d):
        ref = rcv.at[side, 3, d]
        return remote(ref, ref, (core_s.at[d], core_r.at[d]), twin)

    def swap_rows(w):
        @pl.loop(1, 16)
        def _(i):
            a2a_in(w, (plane + 16 - i) % 16).wait_recv()

        all_copy(core, w).start()

    pl.loop(0, 3)(swap_rows)

    @pl.loop(0, PARTS)
    def _(part):
        @pl.when(x <= 2)
        def _():
            r2_copy(1, part).wait_recv()
            dkv[x, part] += xr2[1, part].astype(F32)

            @pl.when((x == 0) | ((x == 1) & (part < 2)))
            def _():
                r2_copy(0, part).wait_recv()
                dkv[x, part] += xr2[0, part].astype(F32)

            z_spread(part)

        @pl.when((part >= 2) | ((x == 3) & (part >= 1)))
        def _():
            z_relay(jnp.where(x == 3, part - 1, part - 2))

    pl.when(x <= 2)(lambda: z_relay(PARTS - 2))
    pl.when(x >= 1)(lambda: z_relay(PARTS - 1))
    core_copy(core, plane).start()

    @pl.loop(1, 16)
    def _(i):
        d = (plane + 16 - i) % 16
        a2a_in(3, d).wait_recv()
        core_copy(core, d).start()

    pl.when(x == 0)(lambda: z_relay(PARTS - 1))

    @pl.loop(1, 3)
    def _(w):
        all_copy(1 - core, w).wait_recv()

    expert_group(1)

    @pl.loop(0, 16)
    def _(i):
        core_copy(1 - core, (plane + 16 - i) % 16).wait_recv()

    all_copy(1 - core, 0).wait_recv()
    expert_group(0)

    goal = lax.broadcasted_iota(jnp.int32, (PACK, PACK), 0)
    have = lax.broadcasted_iota(jnp.int32, (PACK, PACK), 1)
    have_row = have % 4
    have_spot = jnp.where(have < FEW, have_row + 6, have_row + jnp.where(have_row < 2, 4, 8))
    fits = (goal // NL == have % FEW // 4) & (goal % NL == (zl + have_spot) % NL)
    order = jnp.where(fits, 1.0, 0.0).astype(BF16)

    @pl.loop(0, 4)
    def _(i):
        outs = []
        for n in range(4):
            at_rows = pl.ds(pl.multiple_of((i * 4 + n) * FEW, 8), FEW)
            both = [sums[0, at_rows, :], sums[1, at_rows, :]]
            outs.append(dot_nn(order, jnp.concatenate(both, axis=0).astype(BF16)))
        for n in range(SLOTS):
            parts = [out[n * NL : (n + 1) * NL, :] for out in outs]
            here = pl.ds(pl.multiple_of(i * 4 * NL, 4 * NL), 4 * NL)
            hid_ref[n, here, :] = jnp.concatenate(parts, axis=0).astype(BF16)

    @pl.loop(0, PARTS)
    def _(part):
        own = dkv[x, part, block_rows(zl), :]
        for i in range(1, 4):
            n = (mine + i) % 4
            rz_got(part, n).wait_recv()
            own += zr[part, n].astype(F32)
        here = pl.ds(pl.multiple_of(part * SLICE, SLICE), SLICE)
        dk_ref[here, :] = (own[:, :HEAD_DIM] * SCALE).astype(BF16)
        dv_ref[here, :] = own[:, HEAD_DIM:].astype(BF16)

    @pl.loop(0, NL)
    def _(s):
        @pl.when((zl < NL - 1) & (zl - s >= 0))
        def _():
            kz_copy(0, s, zl - s).wait_send()

        @pl.when((zl > 0) & (zl + s < NL))
        def _():
            kz_copy(1, s, zl + s).wait_send()

        ring(0, 0, s, "wait_send")
        ring(1, 1, s, "wait_send")

        @pl.when(s < NL - 1)
        def _():
            ring(0, 1, s, "wait_send")
            ring(1, 0, s, "wait_send")

        @pl.when(x <= 2)
        def _():
            xf_copy(x, s).wait_send()

        @pl.when(x == 0)
        def _():
            xb_copy(0, x, s).wait_send()

        @pl.when(x <= 1)
        def _():
            xb_copy(1, x, s).wait_send()

        @pl.when((x == 1) | (x == 2))
        def _():
            xh_copy(x - 1, s).wait_send()

        @pl.when((x == 3) | (x == 0))
        def _():
            xt_copy((x + 1) % NX, s).wait_send()

    @pl.loop(0, 3)
    def _(w):
        all_copy(core, w).wait_send()

    core_copy(core, plane).wait_send()

    @pl.loop(0, 15)
    def _(r):
        for w in range(4):
            a2a_out(w, r).wait_send()
        core_copy(core, (plane + r + 1) % 16).wait_send()

    @pl.loop(0, 4)
    def _(part):
        @pl.when(x >= 2)
        def _():
            pl.when(part < 2)(lambda: r1_copy(0, part).wait_send())
            pl.when(part >= 2)(lambda: r1_copy(1, part).wait_send())

        @pl.when(x >= 1)
        def _():
            r2_copy(1, part).wait_send()

        @pl.when((x == 3) | ((x == 0) & (part < 2)))
        def _():
            r2_copy(0, part).wait_send()

    @pl.loop(0, PARTS)
    def _(part):
        pair_copy(part).wait_send()

        @pl.loop(1, 4)
        def _(i):
            rz_send(part, (mine + i) % 4).wait_send()


def place(*refs):
    for source, target in zip(refs[:4], refs[4:]):
        target[...] = source[...]


def per_device(queries, keys, values, out_grad, mixed_grad, expert_ids, combine, w_down):
    vmem = pl.BlockSpec(memory_space=pltpu.VMEM)
    dma = pltpu.SemaphoreType.DMA
    hid = w_down.shape[1]
    shapes = (
        jax.ShapeDtypeStruct((TOK, ROWS), BF16),
        jax.ShapeDtypeStruct((TOK, HEAD_DIM), BF16),
        jax.ShapeDtypeStruct((TOK, HEAD_DIM), BF16),
        jax.ShapeDtypeStruct((SLOTS, EXPERTS, hid), BF16),
    )
    scratch = [
        pltpu.VMEM((NX * NL, TOK, WIDE), BF16),
        pltpu.VMEM((NZ, SIDE + TOK, PART), BF16),
        pltpu.VMEM((2, 16, FEW, PART), F32),
        pltpu.VMEM((4, 16, PACK, PART // 2), BF16),
        pltpu.VMEM((2, 4, 16, PACK, PART // 2), BF16),
        pltpu.VMEM((2, 16 * FEW, hid), F32),
        pltpu.VMEM((ROWS, HEAD_DIM), BF16),
        pltpu.VMEM((ROWS, HEAD_DIM), BF16),
        pltpu.VMEM((8, ROWS), F32),
        pltpu.VMEM((HEAD_DIM, ROWS), F32),
        pltpu.VMEM((NX, PARTS, CHUNK, WIDE), F32),
        pltpu.VMEM((4, CHUNK, WIDE), BF16),
        pltpu.VMEM((4, CHUNK, WIDE), BF16),
        pltpu.VMEM((2, 4, CHUNK, WIDE), BF16),
        pltpu.VMEM((2, 4, CHUNK, WIDE), BF16),
        pltpu.VMEM((PARTS, 4, SLICE, WIDE), BF16),
        pltpu.VMEM((PARTS, 4, SLICE, WIDE), BF16),
        pltpu.VMEM((PARTS, 4, SLICE, WIDE), BF16),
        pltpu.VMEM((PARTS, 4, SLICE, WIDE), BF16),
    ]
    for shape in (
        (2, 2, NL), (2, NL), (NL,), (NL,), (2, NL), (NL,),
        (4, 16), (3,), (16,), (4,), (2, 4), (PARTS,), (PARTS, 4),
    ):
        scratch += [dma(shape), dma(shape)]
    dq, dk, dv, hidden = pl.pallas_call(
        kernel,
        out_shape=shapes,
        in_specs=[vmem] * 8,
        out_specs=(vmem,) * 4,
        scratch_shapes=scratch,
        compiler_params=pltpu.CompilerParams(
            collective_id=0, has_side_effects=True, vmem_limit_bytes=56 * 1024 * 1024
        ),
        name="layer_backward",
    )(queries[0], out_grad[0], keys[0], values[0], mixed_grad, expert_ids.T, combine.T, w_down[0])
    dq, dk, dv, hidden = pl.pallas_call(
        place,
        out_shape=shapes,
        in_specs=[vmem] * 4,
        out_specs=(vmem,) * 4,
        name="place_outputs",
    )(dq, dk, dv, hidden)
    return dq[None], dk[None], dv[None], hidden.transpose(1, 0, 2)[None]


def solution(mesh):
    placed = (
        P("dp", "ctx", "tp"),
        P("dp", "ctx", "tp"),
        P("dp", "ctx", "tp"),
        P("dp", "ctx", "tp"),
        P(("dp", "ctx"), "tp"),
        P(("dp", "ctx"), None),
        P(("dp", "ctx"), None),
        P(("dp", "ctx"), "tp", None),
    )
    return jax.shard_map(
        per_device,
        mesh=mesh,
        in_specs=placed,
        out_specs=(
            P("dp", "ctx", "tp"),
            P("dp", "ctx", "tp"),
            P("dp", "ctx", "tp"),
            P(("dp", "ctx"), None, None, "tp"),
        ),
        check_vma=False,
    )
```

```python
import functools
import math

import jax
import jax.numpy as jnp
from jax import lax
from jax.experimental import pallas as pl
from jax.experimental.pallas import tpu as pltpu
from jax.sharding import PartitionSpec as P

MESH = pl.DeviceIdType.MESH
HEAD_DIM = 128
GROUP = 8
TOK = 128
SLOTS = 10
EXPERTS = 128
NX, NY, NL, NZ = 4, 4, 8, 16
RUN = NL * TOK
WIDE = 2 * HEAD_DIM
PARTS = 4
SLICE = TOK // PARTS
CHUNK = RUN // PARTS
ROWS = GROUP * TOK
PACK = NL * SLOTS
SIDE = 16
PART = 512
FEW = 4 * SLOTS
SCALE = HEAD_DIM**-0.5
SCALE2 = SCALE / math.log(2.0)
MASKED = -1e30
F32, BF16 = jnp.float32, jnp.bfloat16


def dot_nt(a, b):
    return lax.dot_general(a, b, (((1,), (1,)), ((), ())), preferred_element_type=F32)


def dot_nn(a, b):
    return lax.dot_general(a, b, (((1,), (0,)), ((), ())), preferred_element_type=F32)


def dot_tn(a, b):
    return lax.dot_general(a, b, (((0,), (0,)), ((), ())), preferred_element_type=F32)


def remote(src, dst, sems, where):
    return pltpu.make_async_remote_copy(
        src_ref=src,
        dst_ref=dst,
        send_sem=sems[0],
        recv_sem=sems[1],
        device_id=where,
        device_id_type=MESH,
    )


def token_targets(ids, weights):
    expert = lax.broadcasted_iota(jnp.int32, (EXPERTS, TOK), 0).astype(F32)
    hits = jnp.zeros((EXPERTS, TOK), F32)
    for k in range(8):
        hits += jnp.where(ids[k : k + 1, :] == expert, 1.0, 0.0)
    rows = lax.broadcasted_iota(jnp.int32, (TOK, TOK), 0)
    cols = lax.broadcasted_iota(jnp.int32, (TOK, TOK), 1)
    before = jnp.where(rows < cols, 1.0, 0.0).astype(BF16)
    ranks = dot_nn(hits.astype(BF16), before)
    slots = [
        jnp.sum(jnp.where(ids[k : k + 1, :] == expert, ranks, 0.0), axis=0, keepdims=True)
        for k in range(8)
    ]
    slots = jnp.concatenate(slots, axis=0)
    top = jnp.concatenate([ids, slots, weights, jnp.zeros_like(ids)], axis=1)
    return jnp.concatenate([top, jnp.zeros_like(top)], axis=0).astype(BF16)


def kernel(
    q_ref, do_ref, k_ref, v_ref, mg_ref, ids_ref, comb_ref, w_ref,
    dq_ref, dk_ref, dv_ref, hid_ref,
    kv, rows, picks, snd, rcv, sums, qs, dos, stat, dqt, dkv, xs1, xr1, xs2, xr2, zs, za, zb, zr,
    ring_s, ring_r, kz_s, kz_r, xf_s, xf_r, xh_s, xh_r, xb_s, xb_r, xt_s, xt_r,
    a2a_s, a2a_r, all_s, all_r, core_s, core_r, r1_s, r1_r, r2_s, r2_r, za_s, za_r, rz_s, rz_r,
):
    y = lax.axis_index("dp")
    c = lax.axis_index("ctx")
    tp = lax.axis_index("tp")
    x, zl = c // NL, c % NL
    zh, core = tp // 2, tp % 2
    z = zh * NL + zl
    plane = y * NX + x

    def at(ax, ay, az, acore):
        return (ay, ax * NL + az % NL, (az // NL) * 2 + acore)

    z_up = at(x, y, (z + 1) % NZ, core)
    z_down = at(x, y, (z + NZ - 1) % NZ, core)
    x_up = at((x + 1) % NX, y, z, core)
    x_down = at((x + NX - 1) % NX, y, z, core)
    twin = at(x, y, z, 1 - core)

    def plane_dev(d):
        return at(d % NX, d // NX, z, core)

    def line_dev(j):
        return at(x, y, zh * NL + j, core)

    barrier = pltpu.get_barrier_semaphore()

    def greet(where):
        pl.semaphore_signal(barrier, inc=1, device_id=where, device_id_type=MESH)

    greet(z_up)
    greet(z_down)
    greet(twin)

    @pl.loop(1, 16)
    def _(i):
        greet(plane_dev((plane + i) % 16))

    @pl.loop(1, NL)
    def _(i):
        greet(line_dev((zl + i) % NL))

    kv[c, :, :HEAD_DIM] = k_ref[...]
    kv[c, :, HEAD_DIM:] = v_ref[...]
    pl.semaphore_wait(barrier, 3 + 15 + 7)

    half = (pl.ds(0, TOK // 2), pl.ds(TOK // 2, TOK // 2))
    whole = pl.ds(0, SIDE + TOK // 2)
    piece = (pl.ds(SIDE, TOK // 2), pl.ds(SIDE + TOK // 2, TOK // 2))

    def ring(way, part, s, op):
        near = (8 - s, 8 + s)[way]
        far = (7 - s, (9 + s) % NZ)[way]
        last = (3, 2)[way]

        def copy(span):
            if op != "wait_recv":
                source, target = rows.at[near, span], rows.at[far, span]
            else:
                source, target = rows.at[far, span], rows.at[far, span]
            sems = (ring_s.at[way, part, s], ring_r.at[way, part, s])
            getattr(remote(source, target, sems, (z_up, z_down)[way]), op)()

        if part == 1:
            copy(piece[1])
        else:
            pl.when(s <= last)(lambda: copy(whole))
            pl.when(s > last)(lambda: copy(piece[0]))

    def kz_copy(way, step, src):
        ref = kv.at[x * NL + src]
        return remote(ref, ref, (kz_s.at[way, step], kz_r.at[way, step]), (z_up, z_down)[way])

    def xf_copy(g, j):
        ref = kv.at[g * NL + j]
        return remote(ref, ref, (xf_s.at[j], xf_r.at[j]), x_up)

    def xh_copy(g, j):
        ref = kv.at[g * NL + j, half[0]]
        return remote(ref, ref, (xh_s.at[j], xh_r.at[j]), x_up)

    def xb_copy(part, g, j):
        ref = kv.at[g * NL + j, half[part]]
        return remote(ref, ref, (xb_s.at[part, j], xb_r.at[part, j]), x_down)

    def xt_copy(g, j):
        ref = kv.at[g * NL + j, half[1]]
        return remote(ref, ref, (xt_s.at[j], xt_r.at[j]), x_down)

    def x_send(j):
        @pl.when(x <= 2)
        def _():
            xf_copy(x, j).start()

        @pl.when(x == 0)
        def _():
            xb_copy(0, x, j).start()

        @pl.when(x <= 1)
        def _():
            xb_copy(1, x, j).start()

    lane = lax.broadcasted_iota(jnp.int32, (1, ROWS), 1) % TOK

    def scores(slot, count, first):
        size = count * TOK
        block = kv[pl.ds(slot, count)].reshape(size, WIDE)
        keys, values = block[:, :HEAD_DIM], block[:, HEAD_DIM:]
        s = dot_nt(keys, qs[...]) * SCALE2
        if first is not None:
            place = lax.broadcasted_iota(jnp.int32, (size, ROWS), 0)
            s = jnp.where(place <= lane + first, s, MASKED)
        return keys, s, dot_nt(values, dos[...])

    def stats(slot, count, first=None):
        _, s, dp = scores(slot, count, first)
        top = stat[0:1, :]
        new_top = jnp.maximum(top, jnp.max(s, axis=0, keepdims=True))
        e = jnp.exp2(s - new_top)
        shrink = jnp.exp2(top - new_top)
        stat[0:1, :] = new_top
        stat[1:2, :] = stat[1:2, :] * shrink + jnp.sum(e, axis=0, keepdims=True)
        stat[2:3, :] = stat[2:3, :] * shrink + jnp.sum(e * dp, axis=0, keepdims=True)

    def x_pass(j):
        @pl.when((j >= 0) & (j < NL))
        def _():
            @pl.when(x >= 1)
            def _():
                xf_copy(x - 1, j).wait_recv()

            @pl.when((x == 1) | (x == 2))
            def _():
                xh_copy(x - 1, j).start()

            @pl.when(x == 3)
            def _():
                xb_copy(0, 0, j).wait_recv()

            @pl.when((x == 3) | (x == 0))
            def _():
                xb_copy(1, (x + 1) % NX, j).wait_recv()
                xt_copy((x + 1) % NX, j).start()

            @pl.when(x >= 1)
            def _():
                stats((x - 1) * NL + j, 1)

            @pl.when(x == 3)
            def _():
                stats(j, 1)

    pick_row = lax.broadcasted_iota(jnp.int32, (16, TOK), 0)
    pick_sub = lax.broadcasted_iota(jnp.int32, (8, TOK), 0)

    def window(w):
        first = jnp.where(w == 0, 6, jnp.where(w == 1, 4, jnp.where(w == 2, 12, 14)))
        return first, (first + jnp.where(w == 0, 2, jnp.where(w == 3, 2, 6))) % NZ

    def make_pick(w, r):
        d = (plane + r + 1) % 16
        expert = (d // NX) * (NX * NL) + (d % NX) * NL + zl
        key = jnp.where(pick_row < SLOTS, expert * SLOTS + pick_row, -1).astype(F32)
        start = window(w)
        columns = []
        for j in range(4):
            named = rows[start[j // 2] + j % 2, pl.ds(0, SIDE), :].astype(F32)
            target = named[:8, :TOK] * float(SLOTS) + named[:8, TOK : 2 * TOK]
            weight = named[:8, 2 * TOK : 3 * TOK]
            chosen = jnp.zeros((16, TOK), F32)
            for k in range(8):
                chosen += jnp.where(target[k : k + 1, :] == key, weight[k : k + 1, :], 0.0)
            column = [
                jnp.where(pick_sub == j, chosen[i : i + 1, :], 0.0)
                + jnp.where(pick_sub == 4 + j, chosen[i + 1 : i + 2, :], 0.0)
                for i in range(0, SLOTS, 2)
            ]
            columns.append(jnp.concatenate(column, axis=0))
        picks[w, r] = jnp.concatenate(columns, axis=1)

    def a2a_out(w, r):
        return remote(
            snd.at[w, r], rcv.at[core, w, plane], (a2a_s.at[w, r], a2a_r.at[w, plane]),
            plane_dev((plane + r + 1) % 16),
        )

    def a2a_in(w, d):
        return remote(
            snd.at[w, 0], rcv.at[core, w, d], (a2a_s.at[w, 0], a2a_r.at[w, d]), plane_dev(d)
        )

    def pack_rows(w, n):
        @pl.when(w < 2)
        def _():
            @pl.loop(0, 8)
            def _(i):
                make_pick(w, n * 8 + i)

        group = jnp.where(w < 2, w, 3 - w)
        total = jnp.zeros((8 * FEW, PART), F32)
        for m, start in enumerate(window(w)):
            source = rows[pl.ds(start, 2), SIDE:, :].reshape(2 * TOK, PART)
            chosen = picks[group, pl.ds(n * 8, 8), :, m * 2 * TOK : (m + 1) * 2 * TOK]
            total += dot_nn(chosen.reshape(8 * FEW, 2 * TOK).astype(BF16), source)
        for i in range(8):
            mine = total[i * FEW : (i + 1) * FEW]
            mine = jnp.concatenate([mine[:, : PART // 2], mine[:, PART // 2 :]], axis=0)
            snd[w, n * 8 + i] = mine.astype(BF16)

        @pl.when(n == 1)
        def _():
            rcv[core, w, plane] = snd[w, 15]

    def launch_rows(w, n):
        @pl.loop(0, 8)
        def _(i):
            @pl.when(n * 8 + i < 15)
            def _():
                a2a_out(w, n * 8 + i).start()

    @pl.when(zl < NL - 1)
    def _():
        kz_copy(0, 0, zl).start()

    @pl.when(zl > 0)
    def _():
        kz_copy(1, 0, zl).start()

    x_send(zl)
    rows[8, pl.ds(SIDE, TOK), :] = mg_ref[...]
    rows[8, pl.ds(0, SIDE), :] = token_targets(
        ids_ref[...].astype(F32), comb_ref[...].astype(F32)
    )
    for h in range(GROUP):
        qs[pl.ds(h * TOK, TOK), :] = q_ref[:, h * HEAD_DIM : (h + 1) * HEAD_DIM]
        dos[pl.ds(h * TOK, TOK), :] = do_ref[:, h * HEAD_DIM : (h + 1) * HEAD_DIM]
    stat[0:1, :] = jnp.full((1, ROWS), MASKED, F32)
    stat[1:3, :] = jnp.zeros((2, ROWS), F32)
    ring(0, 0, 0, "start")
    ring(1, 1, 0, "start")
    ring(0, 1, 0, "start")
    ring(1, 0, 0, "start")
    stats(c, 1, 0)

    @pl.loop(0, NL)
    def _(s):
        below, above = zl - 1 - s, zl + 1 + s

        @pl.when(below >= 0)
        def _():
            kz_copy(0, s, below).wait_recv()

            @pl.when(zl < NL - 1)
            def _():
                kz_copy(0, s + 1, below).start()

        @pl.when(above < NL)
        def _():
            kz_copy(1, s, above).wait_recv()

            @pl.when(zl > 0)
            def _():
                kz_copy(1, s + 1, above).start()

        @pl.when(below >= 0)
        def _():
            x_send(below)

        @pl.when(above < NL)
        def _():
            x_send(above)

        @pl.when(below >= 0)
        def _():
            stats(x * NL + below, 1)

        for way, part in ((0, 0), (1, 1), (0, 1), (1, 0)):
            most = NL if way == part else NL - 1

            @pl.when(s >= 1)
            def _():
                ring(way, part, s - 1, "wait_recv")

                @pl.when(s < most)
                def _():
                    ring(way, part, s, "start")

        @pl.when(s == 1)
        def _():
            x_pass(zl)

        @pl.when(s >= 1)
        def _():
            x_pass(zl - s)
            x_pass(zl + s)

        @pl.when(s >= 2)
        def _():
            pack_rows((s - 2) // 2, s % 2)

        @pl.when((s >= 2) & (s < 6))
        def _():
            launch_rows((s - 2) // 2, s % 2)

    @pl.loop(0, 2)
    def _(n):
        launch_rows(2, n)

    @pl.when(x == 0)
    def _():
        ring(0, 0, NL - 1, "wait_recv")
        ring(1, 1, NL - 1, "wait_recv")

        @pl.loop(0, 2)
        def _(n):
            pack_rows(3, n)
            launch_rows(3, n)

    @pl.when(x >= 2)
    def _():
        @pl.loop(0, NL)
        def _(j):
            xh_copy(x - 2, j).wait_recv()
            xt_copy(x - 2, j).wait_recv()

        @pl.loop(0, 2)
        def _(i):
            stats((x - 2) * NL + i * 4, 4)

    stat[2:3, :] = stat[2:3, :] / stat[1:2, :]
    stat[0:1, :] = stat[0:1, :] + jnp.log2(stat[1:2, :])
    dqt[...] = jnp.zeros_like(dqt)
    def grads(g, part, masked=False):
        here = pl.ds(pl.multiple_of(part * SLICE, SLICE), SLICE)
        block = kv[pl.ds(g * NL, NL), here, :].reshape(CHUNK, WIDE)
        keys, values = block[:, :HEAD_DIM], block[:, HEAD_DIM:]
        s = dot_nt(keys, qs[...]) * SCALE2
        if masked:
            row = lax.broadcasted_iota(jnp.int32, (CHUNK, ROWS), 0)
            place = row // SLICE * TOK + row % SLICE
            s = jnp.where(place <= lane + (zl * TOK - part * SLICE), s, MASKED)
        dp = dot_nt(values, dos[...])
        p = jnp.exp2(s - stat[0:1, :])
        ds = (p * (dp - stat[2:3, :])).astype(BF16)
        dkv[g, part, :, HEAD_DIM:] = dot_nn(p.astype(BF16), dos[...])
        dkv[g, part, :, :HEAD_DIM] = dot_nn(ds, qs[...])
        dqt[...] += dot_tn(keys, ds)

    def r1_copy(way, part):
        return remote(
            xs1.at[part], xr1.at[part], (r1_s.at[part], r1_r.at[part]), (x_up, x_down)[way]
        )

    def r2_copy(way, part, src=None):
        ref = xs2.at[way, part] if src is None else src
        return remote(
            ref, xr2.at[way, part], (r2_s.at[way, part], r2_r.at[way, part]), (x_up, x_down)[way]
        )

    side, mine = zl % 2, zl // 2

    def block_rows(j):
        return pl.ds(pl.multiple_of(j * SLICE, SLICE), SLICE)

    def pair_copy(part):
        sems = (za_s.at[part], za_r.at[part])
        return remote(zs.at[part], za.at[part], sems, line_dev(zl + 1 - 2 * side))

    def rz_send(part, n):
        return remote(
            zb.at[part, n], zr.at[part, mine], (rz_s.at[part, n], rz_r.at[part, mine]),
            line_dev(2 * n + side),
        )

    def rz_got(part, n):
        return remote(
            zb.at[part, n], zr.at[part, n], (rz_s.at[part, n], rz_r.at[part, n]),
            line_dev(2 * n + side),
        )

    def z_spread(part):
        for n in range(4):
            zs[part, n] = dkv[x, part, block_rows(2 * n + 1 - side), :].astype(BF16)
        pair_copy(part).start()

    def z_relay(part):
        pair_copy(part).wait_recv()
        for n in range(4):
            total = dkv[x, part, block_rows(2 * n + side), :] + za[part, n].astype(F32)
            dkv[x, part, block_rows(2 * n + side), :] = total
            zb[part, n] = total.astype(BF16)

        @pl.loop(1, 4)
        def _(i):
            rz_send(part, (mine + i) % 4).start()

    @pl.when(x >= 2)
    def _():
        @pl.loop(0, 4)
        def _(part):
            grads(x - 2, part)
            xs1[part] = dkv[x - 2, part].astype(BF16)
            pl.when(part < 2)(lambda: r1_copy(0, part).start())
            pl.when(part >= 2)(lambda: r1_copy(1, part).start())

    @pl.when(x == 3)
    def _():
        @pl.loop(0, 4)
        def _(n):
            part = (n + 2) % 4
            grads(0, part)

            @pl.when(part < 2)
            def _():
                r1_copy(0, part).wait_recv()
                dkv[0, part] += xr1[part].astype(F32)

            xs2[0, part] = dkv[0, part].astype(BF16)
            r2_copy(0, part).start()

    @pl.when(x >= 1)
    def _():
        @pl.loop(0, 4)
        def _(part):
            grads(x - 1, part)

            @pl.when((part >= 2) & (x < 3))
            def _():
                r1_copy(1, part).wait_recv()
                dkv[x - 1, part] += xr1[part].astype(F32)

            xs2[1, part] = dkv[x - 1, part].astype(BF16)
            r2_copy(1, part).start()

    @pl.loop(0, 4)
    def _(part):
        grads(x, part, True)
        pl.when(x == 3)(lambda: z_spread(part))

    @pl.when(x >= 1)
    def _():
        ring(0, 0, NL - 1, "wait_recv")
        ring(1, 1, NL - 1, "wait_recv")

        @pl.loop(0, 2)
        def _(n):
            pack_rows(3, n)
            launch_rows(3, n)

    @pl.when(x == 0)
    def _():
        @pl.loop(0, 2)
        def _(part):
            r1_copy(0, part).wait_recv()
            r2_copy(0, part, xr1.at[part]).start()

    for h in range(GROUP):
        at_head = slice(h * TOK, (h + 1) * TOK)
        dq_ref[:, at_head] = (dqt[:, at_head].T * SCALE).astype(BF16)

    def all_copy(side, w):
        ref = rcv.at[side, w]
        return remote(ref, ref, (all_s.at[w], all_r.at[w]), twin)

    row = lax.broadcasted_iota(jnp.int32, (8 * PACK, PART // 2), 0) % 4
    spot = row + jnp.where(row < 2, 4, 8)
    low = ((z + 14 + row) % NZ < NL, (z + 8 + spot) % NZ < NL)

    def expert_group(group):
        @pl.loop(0, 2)
        def _(i):
            total = jnp.zeros((8 * FEW, w_ref.shape[0]), F32)
            for side in range(2):
                near = rcv[side, group, pl.ds(i * 8, 8)].reshape(8 * PACK, PART // 2)
                far = rcv[side, 3 - group, pl.ds(i * 8, 8)].reshape(8 * PACK, PART // 2)
                for part in range(2):
                    a, b = (near, far) if part == 0 else (far, near)
                    left = jnp.where(low[group], a, b).astype(F32)
                    for m in range(2):
                        begin = (part * 2 + side) * PART + m * (PART // 2)
                        cuts = [
                            left[n * PACK + m * FEW : n * PACK + (m + 1) * FEW] for n in range(8)
                        ]
                        total += dot_nt(
                            jnp.concatenate(cuts, axis=0).astype(BF16),
                            w_ref[:, begin : begin + PART // 2],
                        )
            sums[group, pl.ds(pl.multiple_of(i * 8 * FEW, 8), 8 * FEW), :] = total

    def core_copy(side, d):
        ref = rcv.at[side, 3, d]
        return remote(ref, ref, (core_s.at[d], core_r.at[d]), twin)

    def swap_rows(w):
        @pl.loop(1, 16)
        def _(i):
            a2a_in(w, (plane + 16 - i) % 16).wait_recv()

        all_copy(core, w).start()

    pl.loop(0, 3)(swap_rows)

    @pl.loop(0, PARTS)
    def _(part):
        @pl.when(x <= 2)
        def _():
            r2_copy(1, part).wait_recv()
            dkv[x, part] += xr2[1, part].astype(F32)

            @pl.when((x == 0) | ((x == 1) & (part < 2)))
            def _():
                r2_copy(0, part).wait_recv()
                dkv[x, part] += xr2[0, part].astype(F32)

            z_spread(part)

        @pl.when((part >= 2) | ((x == 3) & (part >= 1)))
        def _():
            z_relay(jnp.where(x == 3, part - 1, part - 2))

    pl.when(x <= 2)(lambda: z_relay(PARTS - 2))
    pl.when(x >= 1)(lambda: z_relay(PARTS - 1))
    core_copy(core, plane).start()

    @pl.loop(1, 16)
    def _(i):
        d = (plane + 16 - i) % 16
        a2a_in(3, d).wait_recv()
        core_copy(core, d).start()

    pl.when(x == 0)(lambda: z_relay(PARTS - 1))

    @pl.loop(1, 3)
    def _(w):
        all_copy(1 - core, w).wait_recv()

    expert_group(1)

    @pl.loop(0, 16)
    def _(i):
        core_copy(1 - core, (plane + 16 - i) % 16).wait_recv()

    all_copy(1 - core, 0).wait_recv()
    expert_group(0)

    goal = lax.broadcasted_iota(jnp.int32, (PACK, PACK), 0)
    have = lax.broadcasted_iota(jnp.int32, (PACK, PACK), 1)
    have_row = have % 4
    have_spot = jnp.where(have < FEW, have_row + 6, have_row + jnp.where(have_row < 2, 4, 8))
    fits = (goal // NL == have % FEW // 4) & (goal % NL == (zl + have_spot) % NL)
    order = jnp.where(fits, 1.0, 0.0).astype(BF16)

    @pl.loop(0, 4)
    def _(i):
        outs = []
        for n in range(4):
            at_rows = pl.ds(pl.multiple_of((i * 4 + n) * FEW, 8), FEW)
            both = [sums[0, at_rows, :], sums[1, at_rows, :]]
            outs.append(dot_nn(order, jnp.concatenate(both, axis=0).astype(BF16)))
        for n in range(SLOTS):
            parts = [out[n * NL : (n + 1) * NL, :] for out in outs]
            here = pl.ds(pl.multiple_of(i * 4 * NL, 4 * NL), 4 * NL)
            hid_ref[n, here, :] = jnp.concatenate(parts, axis=0).astype(BF16)

    @pl.loop(0, NL)
    def _(s):
        @pl.when((zl < NL - 1) & (zl - s >= 0))
        def _():
            kz_copy(0, s, zl - s).wait_send()

        @pl.when((zl > 0) & (zl + s < NL))
        def _():
            kz_copy(1, s, zl + s).wait_send()

        ring(0, 0, s, "wait_send")
        ring(1, 1, s, "wait_send")

        @pl.when(s < NL - 1)
        def _():
            ring(0, 1, s, "wait_send")
            ring(1, 0, s, "wait_send")

        @pl.when(x <= 2)
        def _():
            xf_copy(x, s).wait_send()

        @pl.when(x == 0)
        def _():
            xb_copy(0, x, s).wait_send()

        @pl.when(x <= 1)
        def _():
            xb_copy(1, x, s).wait_send()

        @pl.when((x == 1) | (x == 2))
        def _():
            xh_copy(x - 1, s).wait_send()

        @pl.when((x == 3) | (x == 0))
        def _():
            xt_copy((x + 1) % NX, s).wait_send()

    @pl.loop(0, 3)
    def _(w):
        all_copy(core, w).wait_send()

    core_copy(core, plane).wait_send()

    @pl.loop(0, 15)
    def _(r):
        for w in range(4):
            a2a_out(w, r).wait_send()
        core_copy(core, (plane + r + 1) % 16).wait_send()

    @pl.loop(0, 4)
    def _(part):
        @pl.when(x >= 2)
        def _():
            pl.when(part < 2)(lambda: r1_copy(0, part).wait_send())
            pl.when(part >= 2)(lambda: r1_copy(1, part).wait_send())

        @pl.when(x >= 1)
        def _():
            r2_copy(1, part).wait_send()

        @pl.when((x == 3) | ((x == 0) & (part < 2)))
        def _():
            r2_copy(0, part).wait_send()

    @pl.loop(0, PARTS)
    def _(part):
        own = dkv[x, part, block_rows(zl), :]
        for i in range(1, 4):
            n = (mine + i) % 4
            rz_got(part, n).wait_recv()
            own += zr[part, n].astype(F32)
        here = pl.ds(pl.multiple_of(part * SLICE, SLICE), SLICE)
        dk_ref[here, :] = (own[:, :HEAD_DIM] * SCALE).astype(BF16)
        dv_ref[here, :] = own[:, HEAD_DIM:].astype(BF16)

    @pl.loop(0, PARTS)
    def _(part):
        pair_copy(part).wait_send()

        @pl.loop(1, 4)
        def _(i):
            rz_send(part, (mine + i) % 4).wait_send()


def place(*refs):
    for source, target in zip(refs[:4], refs[4:]):
        target[...] = source[...]


def per_device(queries, keys, values, out_grad, mixed_grad, expert_ids, combine, w_down):
    vmem = pl.BlockSpec(memory_space=pltpu.VMEM)
    dma = pltpu.SemaphoreType.DMA
    hid = w_down.shape[1]
    shapes = (
        jax.ShapeDtypeStruct((TOK, ROWS), BF16),
        jax.ShapeDtypeStruct((TOK, HEAD_DIM), BF16),
        jax.ShapeDtypeStruct((TOK, HEAD_DIM), BF16),
        jax.ShapeDtypeStruct((SLOTS, EXPERTS, hid), BF16),
    )
    scratch = [
        pltpu.VMEM((NX * NL, TOK, WIDE), BF16),
        pltpu.VMEM((NZ, SIDE + TOK, PART), BF16),
        pltpu.VMEM((2, 16, FEW, PART), F32),
        pltpu.VMEM((4, 16, PACK, PART // 2), BF16),
        pltpu.VMEM((2, 4, 16, PACK, PART // 2), BF16),
        pltpu.VMEM((2, 16 * FEW, hid), F32),
        pltpu.VMEM((ROWS, HEAD_DIM), BF16),
        pltpu.VMEM((ROWS, HEAD_DIM), BF16),
        pltpu.VMEM((8, ROWS), F32),
        pltpu.VMEM((HEAD_DIM, ROWS), F32),
        pltpu.VMEM((NX, PARTS, CHUNK, WIDE), F32),
        pltpu.VMEM((4, CHUNK, WIDE), BF16),
        pltpu.VMEM((4, CHUNK, WIDE), BF16),
        pltpu.VMEM((2, 4, CHUNK, WIDE), BF16),
        pltpu.VMEM((2, 4, CHUNK, WIDE), BF16),
        pltpu.VMEM((PARTS, 4, SLICE, WIDE), BF16),
        pltpu.VMEM((PARTS, 4, SLICE, WIDE), BF16),
        pltpu.VMEM((PARTS, 4, SLICE, WIDE), BF16),
        pltpu.VMEM((PARTS, 4, SLICE, WIDE), BF16),
    ]
    for shape in (
        (2, 2, NL), (2, NL), (NL,), (NL,), (2, NL), (NL,),
        (4, 16), (3,), (16,), (4,), (2, 4), (PARTS,), (PARTS, 4),
    ):
        scratch += [dma(shape), dma(shape)]
    dq, dk, dv, hidden = pl.pallas_call(
        kernel,
        out_shape=shapes,
        in_specs=[vmem] * 8,
        out_specs=(vmem,) * 4,
        scratch_shapes=scratch,
        compiler_params=pltpu.CompilerParams(
            collective_id=0, has_side_effects=True, vmem_limit_bytes=56 * 1024 * 1024
        ),
        name="layer_backward",
    )(queries[0], out_grad[0], keys[0], values[0], mixed_grad, expert_ids.T, combine.T, w_down[0])
    dq, dk, dv, hidden = pl.pallas_call(
        place,
        out_shape=shapes,
        in_specs=[vmem] * 4,
        out_specs=(vmem,) * 4,
        name="place_outputs",
    )(dq, dk, dv, hidden)
    return dq[None], dk[None], dv[None], hidden.transpose(1, 0, 2)[None]


def solution(mesh):
    placed = (
        P("dp", "ctx", "tp"),
        P("dp", "ctx", "tp"),
        P("dp", "ctx", "tp"),
        P("dp", "ctx", "tp"),
        P(("dp", "ctx"), "tp"),
        P(("dp", "ctx"), None),
        P(("dp", "ctx"), None),
        P(("dp", "ctx"), "tp", None),
    )
    return jax.shard_map(
        per_device,
        mesh=mesh,
        in_specs=placed,
        out_specs=(
            P("dp", "ctx", "tp"),
            P("dp", "ctx", "tp"),
            P("dp", "ctx", "tp"),
            P(("dp", "ctx"), None, None, "tp"),
        ),
        check_vma=False,
    )
```
